512 devices in a mesh: tm: 16 (over z), row: 4 (over y), col: 8 (over x, core).
Axes of the slice: x: 4, y: 4, z: 16, core: 2. Of those that a mesh axis runs over, the one named last changes fastest.
Arguments:
- features: bfloat16 [64, 32, 128, 192], P('tm', 'row', 'col'), may hold values from -6 to 6
- conv_first: bfloat16 [3, 3, 3, 192, 192], replicated, may hold values from -0.078125 to 0.078125
- conv_second: bfloat16 [3, 3, 3, 192, 192], replicated, may hold values from -0.078125 to 0.078125
- gain_first: float32 [192], replicated, may hold values from 0.25 to 1.75
- gain_second: float32 [192], replicated, may hold values from 0.25 to 1.75
Outputs:
- decoded: bfloat16 [64, 32, 128, 192], P('tm', 'row', 'col')
The draws below stay inside these ranges and needn't reach their ends.
All inputs are finite; a program needn't handle non-finite values.
Results may differ from the reference program's by a relative error of at most 0.0043.
Values may be sent and summed in bfloat16 or wider, within the bound.
A program may use at most 128 MiB of HBM per device.

```python
import jax
import jax.numpy as jnp
from jax import lax

C = 192
FRAMES = 64
HEIGHT = 32
BREADTH = 128


def shard_levels(own_key, extent, cuts, smallest, largest):
    factor_of = 1.0
    for axis_at, blocks in cuts:
        draws = jax.random.uniform(jax.random.fold_in(jax.random.fold_in(own_key, 6), axis_at), (blocks,), jnp.float32, smallest / len(cuts), largest / len(cuts))
        factor_of = factor_of * jnp.repeat(jnp.exp(draws), extent[axis_at] // blocks).reshape((-1,) + (1,) * (len(extent) - 1 - axis_at))
    return factor_of


def normal_values(key, extent, width, reach, pieces=(), kind=jnp.bfloat16):
    result = width * jax.random.normal(key, extent, jnp.float32)
    if pieces:
        result = result * shard_levels(key, extent, pieces, -0.22, 0.18)
    return jnp.clip(result, -reach, reach).astype(kind)


def setup_inputs(seed: int = 0) -> dict:
    key_list = jax.random.split(jax.random.key(seed), 6)
    features = normal_values(key_list[0], (FRAMES, HEIGHT, BREADTH, C), 1.0, 6.0, ((0, 16), (1, 4), (2, 8)))
    conv_first = normal_values(key_list[1], (3, 3, 3, C, C), (27 * C) ** -0.5, 0.078125)
    conv_second = normal_values(key_list[2], (3, 3, 3, C, C), (27 * C) ** -0.5, 0.078125)
    gain_first = jnp.clip(1.0 + 0.15 * jax.random.normal(key_list[3], (C,), jnp.float32), 0.25, 1.75)
    gain_second = jnp.clip(1.0 + 0.15 * jax.random.normal(key_list[4], (C,), jnp.float32), 0.25, 1.75)
    return dict(features=features, conv_first=conv_first, conv_second=conv_second, gain_first=gain_first, gain_second=gain_second)


def norm_act(values, gain):
    mean_sq = lax.optimization_barrier(jnp.mean(values * values, axis=-1, keepdims=True))
    return jax.nn.silu(values * lax.rsqrt(mean_sq + 1e-06) * gain)

def conv_valid(padded, weight):
    out_frames = padded.shape[0] - 2
    out_rows = padded.shape[1] - 2
    out_cols = padded.shape[2] - 2
    channels = padded.shape[3]
    stacked = weight.reshape(3, 9 * channels, weight.shape[4])
    summed = jnp.zeros((out_frames * out_rows * out_cols, weight.shape[4]), jnp.float32)
    for frame_tap in range(3):
        window = padded[frame_tap:frame_tap + out_frames]
        patches = jnp.concatenate([window[:, row_tap:row_tap + out_rows, col_tap:col_tap + out_cols, :] for row_tap in range(3) for col_tap in range(3)], axis=-1)
        summed = summed + jnp.dot(patches.reshape(-1, 9 * channels), stacked[frame_tap], preferred_element_type=jnp.float32)
    return summed.reshape(out_frames, out_rows, out_cols, weight.shape[4])

def conv_frames(padded, weight):
    out_frames = padded.shape[0] - 2

    def single(index):
        window = lax.dynamic_slice_in_dim(padded, index, 3, 0)
        return conv_valid(window, weight)[0]
    return lax.map(single, jnp.arange(out_frames, dtype=jnp.int32))

def reference(features, conv_first, conv_second, gain_first, gain_second):
    widened = features.astype(jnp.float32)
    hidden_first = norm_act(widened, gain_first).astype(jnp.bfloat16)
    padded = jnp.pad(hidden_first, ((2, 0), (1, 1), (1, 1), (0, 0)))
    first_out = conv_frames(padded, conv_first)
    hidden_second = norm_act(first_out, gain_second).astype(jnp.bfloat16)
    padded = jnp.pad(hidden_second, ((2, 0), (1, 1), (1, 1), (0, 0)))
    second_out = conv_frames(padded, conv_second)
    return (widened + second_out).astype(jnp.bfloat16)
```

```python
import functools

import jax
import jax.numpy as jnp
from jax import lax
from jax.experimental import pallas as pl
from jax.experimental.pallas import tpu as pltpu
from jax.sharding import PartitionSpec as P

MESH = pl.DeviceIdType.MESH
BF = jnp.bfloat16
F32 = jnp.float32
C = 192
LO = 128
FR, RO, CO = 4, 8, 16
PX = RO * CO
EF, ER, EC = 6, 10, 32
SIDES = ((-1, 0), (1, 0), (0, -1), (0, 1), (-1, -1), (-1, 1), (1, -1), (1, 1))
SPOT = ((0, 48), (48, 48), (96, 32), (128, 32), (160, 16), (176, 16), (192, 16), (208, 16))
RIM = 224
BODY = 3 * PX


def opposite(side):
    dr, dc = SIDES[side]
    return SIDES.index((-dr, -dc))


def at(frame, row, col):
    return (frame * ER + row) * EC + col


def norm_act(low, high, gain_low, gain_high):
    total = jnp.sum(low * low + 0.5 * (high * high), axis=-1, keepdims=True)
    scale = lax.rsqrt(total * (1.0 / C) + 1e-06)

    def silu(values, gain):
        half = 0.5 * (values * scale * gain)
        return half + half * jnp.tanh(half)

    return silu(low, gain_low), silu(high, gain_high)


def twice(high):
    return jnp.concatenate([high, high], axis=-1)


def first_half(shape):
    return lax.broadcasted_iota(jnp.int32, shape, len(shape) - 1) < 64


def swap(value):
    return pltpu.roll(value, 64, 1)


def kernel(sizes, x_hbm, w1_hbm, w2_hbm, g1_hbm, g2_hbm, out_hbm,
           x, gains, wlo, whi, wti, elo, ehi, taps, body_s, body_r, rim_s, rim_r, out,
           load_sem, gain_sem, w_sem, out_sem, body_ss, body_rs, rim_ss, rim_rs, fwd_ss, fwd_rs):
    n_tm, n_row, n_col = sizes
    tm, row, col = (lax.axis_index(name) for name in ("tm", "row", "col"))

    loads = [pltpu.make_async_copy(x_hbm, x, load_sem)]
    for k, g in enumerate((g1_hbm, g2_hbm)):
        loads.append(pltpu.make_async_copy(g, gains.at[k], gain_sem.at[k]))
    for load in loads:
        load.start()
    w_loads = []
    for k, w in enumerate((w1_hbm, w2_hbm)):
        group = [
            pltpu.make_async_copy(w.at[:, :, :, 0:128, :], wlo.at[k], w_sem.at[k, 0]),
            pltpu.make_async_copy(w.at[:, :, 0:2, 128:192, :], whi.at[k], w_sem.at[k, 1]),
            pltpu.make_async_copy(w.at[:, :, 2, 128:192, :], wti.at[k, :, 0:3], w_sem.at[k, 2]),
        ]
        for load in group:
            load.start()
        w_loads.append(group)

    def neighbour(dr, dc):
        return (tm, lax.rem(row + (dr + n_row), n_row), lax.rem(col + (dc + n_col), n_col))

    later = (lax.rem(tm + 1, n_tm), row, col)
    earlier = (lax.rem(tm + (n_tm - 1), n_tm), row, col)
    barrier = pltpu.get_barrier_semaphore()
    for dr, dc in SIDES:
        pl.semaphore_signal(barrier, inc=1, device_id=neighbour(dr, dc), device_id_type=MESH)
    pl.semaphore_signal(barrier, inc=1, device_id=earlier, device_id_type=MESH)

    wti[:, :, 3] = jnp.zeros((2, 3, 64, C), BF)

    keep = {
        -1: jnp.where(row > 0, 1.0, 0.0),
        1: jnp.where(row < n_row - 1, 1.0, 0.0),
        -2: jnp.where(col > 0, 1.0, 0.0),
        2: jnp.where(col < n_col - 1, 1.0, 0.0),
    }
    keep_tm = jnp.where(tm > 0, 1.0, 0.0)

    def side_keep(side):
        dr, dc = SIDES[side]
        value = 1.0
        if dr:
            value = value * keep[dr]
        if dc:
            value = value * keep[2 * dc]
        return value

    def put_body(k, frame, low, high):
        for r in range(RO):
            elo[k, pl.ds(at(frame, r + 1, 8), CO)] = low[r * CO:(r + 1) * CO]
            ehi[k, pl.ds(at(frame, r + 1, 8), CO)] = high[r * CO:(r + 1) * CO]

    def body_copy(k):
        return pltpu.make_async_remote_copy(
            src_ref=body_s.at[k], dst_ref=body_r.at[k], send_sem=body_ss.at[k], recv_sem=body_rs.at[k],
            device_id=later, device_id_type=MESH)

    def forward_copy(k):
        return pltpu.make_async_remote_copy(
            src_ref=rim_r.at[k, 2], dst_ref=rim_r.at[k, 0], send_sem=fwd_ss.at[k], recv_sem=fwd_rs.at[k],
            device_id=later, device_id_type=MESH)

    def rim_copy(k, pair, side):
        here, size = SPOT[side]
        there, _ = SPOT[opposite(side)]
        return pltpu.make_async_remote_copy(
            src_ref=rim_s.at[k, pair, pl.ds(here, size)], dst_ref=rim_r.at[k, pair + 1, pl.ds(there, size)],
            send_sem=rim_ss.at[k, pair, side], recv_sem=rim_rs.at[k, pair, opposite(side)],
            device_id=neighbour(*SIDES[side]), device_id_type=MESH)

    def rim_wait(k, pair):
        for side in range(8):
            rim_copy(k, pair, side).wait_recv()

    def send_body(k):
        low = [elo[k, pl.ds(at(f, r, 8), CO)] for f in (4, 5) for r in range(1, 9)]
        body_s[k, 0:256] = jnp.concatenate(low, axis=0).astype(BF)
        mask = first_half((CO, LO))
        high = [jnp.where(mask, ehi[k, pl.ds(at(4, r, 8), CO)], ehi[k, pl.ds(at(5, r, 8), CO)]) for r in range(1, 9)]
        body_s[k, 256:384] = jnp.concatenate(high, axis=0).astype(BF)
        body_copy(k).start()

    def send_rims(k, pair):
        f = 2 + 2 * pair
        mask = first_half((CO, LO))
        for side, (dr, dc) in enumerate(SIDES):
            spot, _ = SPOT[side]
            r = 1 if dr < 0 else RO
            c = 8 if dc < 0 else 23
            if dc == 0:
                low = jnp.concatenate([elo[k, pl.ds(at(f + i, r, 8), CO)] for i in range(2)], axis=0)
                high = jnp.where(mask, *[ehi[k, pl.ds(at(f + i, r, 8), CO)] for i in range(2)])
                rim_s[k, pair, spot:spot + 32] = low.astype(BF)
                rim_s[k, pair, spot + 32:spot + 48] = high.astype(BF)
            elif dr == 0:
                low = jnp.concatenate([elo[k, pl.ds(at(f + i, 1, c), RO, stride=EC)] for i in range(2)], axis=0)
                high = jnp.where(mask[:RO], *[ehi[k, pl.ds(at(f + i, 1, c), RO, stride=EC)] for i in range(2)])
                rim_s[k, pair, spot:spot + 16] = low.astype(BF)
                rim_s[k, pair, spot + 16:spot + 32] = jnp.concatenate([high, high], axis=0).astype(BF)
            else:
                lines = lax.broadcasted_iota(jnp.int32, (8, LO), 0)
                value = jnp.zeros((8, LO), F32)
                for i, (ref, frame) in enumerate(((elo, f), (elo, f + 1), (ehi, f), (ehi, f + 1))):
                    line = jnp.broadcast_to(ref[k, pl.ds(at(frame, r, c), 1)], (8, LO))
                    value = jnp.where(lines == i, line, value)
                rim_s[k, pair, spot:spot + 16] = jnp.concatenate([value, value], axis=0).astype(BF)
            rim_copy(k, pair, side).start()

    def put_rims(k, slot):
        f = 2 * slot
        mask = first_half((CO, LO))
        for side, (dr, dc) in enumerate(SIDES):
            spot, _ = SPOT[side]
            r = 0 if dr < 0 else RO + 1
            c = 7 if dc < 0 else 24
            factor = side_keep(side)
            if slot == 0:
                factor = factor * keep_tm
            if dc == 0:
                low = rim_r[k, slot, spot:spot + 32].astype(F32) * factor
                high = rim_r[k, slot, spot + 32:spot + 48].astype(F32) * factor
                other = swap(high)
                for i in range(2):
                    elo[k, pl.ds(at(f + i, r, 8), CO)] = low[i * CO:(i + 1) * CO]
                ehi[k, pl.ds(at(f, r, 8), CO)] = jnp.where(mask, high, other)
                ehi[k, pl.ds(at(f + 1, r, 8), CO)] = jnp.where(mask, other, high)
            elif dr == 0:
                low = rim_r[k, slot, spot:spot + 16].astype(F32) * factor
                high = rim_r[k, slot, spot + 16:spot + 32].astype(F32)[:RO] * factor
                other = swap(high)
                for i in range(2):
                    elo[k, pl.ds(at(f + i, 1, c), RO, stride=EC)] = low[i * RO:(i + 1) * RO]
                ehi[k, pl.ds(at(f, 1, c), RO, stride=EC)] = jnp.where(mask[:RO], high, other)
                ehi[k, pl.ds(at(f + 1, 1, c), RO, stride=EC)] = jnp.where(mask[:RO], other, high)
            else:
                value = rim_r[k, slot, spot:spot + 16].astype(F32)[:8] * factor
                for i in range(2):
                    elo[k, pl.ds(at(f + i, r, c), 1)] = value[i:i + 1]
                    ehi[k, pl.ds(at(f + i, r, c), 1)] = value[i + 2:i + 3]

    def put_earlier(k):
        mask = first_half((PX, LO))
        low = body_r[k, 0:256].astype(F32) * keep_tm
        high = body_r[k, 256:384].astype(F32) * keep_tm
        other = swap(high)
        put_body(k, 0, low[:PX], jnp.where(mask, high, other))
        put_body(k, 1, low[PX:], jnp.where(mask, other, high))

    def build(k, frame):
        mask = first_half((CO, LO))

        def line(r, _):
            low = [elo[k, pl.ds(at(frame, r, 7 + c), CO)] for c in range(3)]
            high = [ehi[k, pl.ds(at(frame, r, 7 + c), CO)] for c in range(3)]
            below = ehi[k, pl.ds(at(frame, min(r + 1, ER - 1), 9), CO)]
            lines = pl.ds(r * CO, CO)
            for c in range(3):
                taps[k, frame, lines, c * LO:(c + 1) * LO] = low[c].astype(BF)
            taps[k, frame, lines, 3 * LO:4 * LO] = jnp.where(mask, high[0], high[1]).astype(BF)
            taps[k, frame, lines, 4 * LO:5 * LO] = jnp.where(mask, high[2], below).astype(BF)

        for r in range(ER):
            line(r, None)

    def conv(k, frame):
        total = None
        for a in range(3):
            f = frame - 2 + a
            left = [taps[k, f:f + 2, b * CO:b * CO + PX, 0:4 * LO].reshape(2 * PX, 4 * LO) for b in range(3)]
            left += [taps[k, f:f + 2, b * CO:b * CO + PX, 4 * LO:5 * LO].reshape(2 * PX, LO) for b in (0, 2)]
            right = []
            for b in range(3):
                right += [wlo[k, a, b].reshape(3 * LO, C), whi[k, a, b].reshape(LO, C)]
            right.append(wti[k, a].reshape(2 * LO, C))
            part = jnp.dot(jnp.concatenate(left, axis=1), jnp.concatenate(right, axis=0), preferred_element_type=F32)
            total = part if total is None else total + part
        return total

    for load in loads:
        load.wait()
    gain = []
    for k in range(2):
        value = gains[k]
        gain.append((value[:, :LO], twice(value[:, LO:])))
    for f in (2, 3, 0, 1):
        value = x[f].reshape(PX, C).astype(F32)
        put_body(0, f + 2, *norm_act(value[:, :LO], twice(value[:, LO:]), *gain[0]))

    pl.semaphore_wait(barrier, 9)
    send_rims(0, 1)
    send_rims(0, 0)
    send_body(0)

    def finish_first(frame):
        total = conv(0, frame)
        low, high = norm_act(total[:, :LO], twice(total[:, LO:]), *gain[1])
        for i in range(2):
            put_body(1, frame + i, low[i * PX:(i + 1) * PX], high[i * PX:(i + 1) * PX])

    def finish_second(frame):
        f = frame - 2
        total = conv(1, frame) + x[f:f + 2].reshape(2 * PX, C).astype(F32)
        out[f:f + 2] = total.astype(BF).reshape(2, RO, CO, C)
        pltpu.make_async_copy(out.at[f:f + 2], out_hbm.at[f:f + 2], out_sem.at[f // 2]).start()

    rim_wait(0, 1)
    forward_copy(0).start()
    put_rims(0, 2)
    build(0, 4)
    build(0, 5)
    rim_wait(0, 0)
    put_rims(0, 1)
    build(0, 2)
    build(0, 3)
    for load in w_loads[0]:
        load.wait()
    finish_first(4)
    send_rims(1, 1)
    send_body(1)

    body_copy(0).wait_recv()
    forward_copy(0).wait_recv()
    put_earlier(0)
    put_rims(0, 0)
    build(0, 0)
    build(0, 1)
    finish_first(2)
    send_rims(1, 0)

    rim_wait(1, 1)
    forward_copy(1).start()
    put_rims(1, 2)
    build(1, 4)
    build(1, 5)
    rim_wait(1, 0)
    put_rims(1, 1)
    build(1, 2)
    build(1, 3)
    for load in w_loads[1]:
        load.wait()
    finish_second(4)

    body_copy(1).wait_recv()
    forward_copy(1).wait_recv()
    put_earlier(1)
    put_rims(1, 0)
    build(1, 0)
    build(1, 1)
    finish_second(2)

    for k in range(2):
        body_copy(k).wait_send()
        forward_copy(k).wait_send()
        for pair in range(2):
            for side in range(8):
                rim_copy(k, pair, side).wait_send()
    for f in (2, 0):
        pltpu.make_async_copy(out.at[f:f + 2], out_hbm.at[f:f + 2], out_sem.at[f // 2]).wait()


def solution(mesh):
    sizes = tuple(mesh.shape[name] for name in ("tm", "row", "col"))

    def shards(features, conv_first, conv_second, gain_first, gain_second):
        anywhere = pl.BlockSpec(memory_space=pl.ANY)
        dma = pltpu.SemaphoreType.DMA
        return pl.pallas_call(
            functools.partial(kernel, sizes),
            out_shape=jax.ShapeDtypeStruct(features.shape, BF),
            in_specs=[anywhere] * 5,
            out_specs=anywhere,
            scratch_shapes=[
                pltpu.VMEM((FR, RO, CO, C), BF),
                pltpu.VMEM((2, 1, C), F32),
                pltpu.VMEM((2, 3, 3, 3, LO, C), BF),
                pltpu.VMEM((2, 3, 3, 2, 64, C), BF),
                pltpu.VMEM((2, 3, 4, 64, C), BF),
                pltpu.VMEM((2, EF * ER * EC, LO), F32),
                pltpu.VMEM((2, EF * ER * EC, LO), F32),
                pltpu.VMEM((2, EF, ER * CO, 5 * LO), BF),
                pltpu.VMEM((2, BODY, LO), BF),
                pltpu.VMEM((2, BODY, LO), BF),
                pltpu.VMEM((2, 2, RIM, LO), BF),
                pltpu.VMEM((2, 3, RIM, LO), BF),
                pltpu.VMEM((FR, RO, CO, C), BF),
                dma, dma((2,)), dma((2, 3)), dma((2,)),
                dma((2,)), dma((2,)), dma((2, 2, 8)), dma((2, 2, 8)), dma((2,)), dma((2,)),
            ],
            compiler_params=pltpu.CompilerParams(
                collective_id=0, has_side_effects=True, vmem_limit_bytes=48 * 1024 * 1024),
        )(features, conv_first, conv_second, gain_first.reshape(1, C), gain_second.reshape(1, C))

    return jax.shard_map(
        shards, mesh=mesh, in_specs=(P("tm", "row", "col", None), P(), P(), P(), P()),
        out_specs=P("tm", "row", "col", None), check_vma=False)
```

```python
import functools

import jax
import jax.numpy as jnp
from jax import lax
from jax.experimental import pallas as pl
from jax.experimental.pallas import tpu as pltpu
from jax.sharding import PartitionSpec as P

MESH = pl.DeviceIdType.MESH
BF = jnp.bfloat16
F32 = jnp.float32
C = 192
LO = 128
FR, RO, CO = 4, 8, 16
PX = RO * CO
EF, ER1, ER2, EC = 6, 12, 10, 32
MAIN, SIDE = ER2 * CO, 2 * CO
SIDES = ((-1, 0), (1, 0), (0, -1), (0, 1), (-1, -1), (-1, 1), (1, -1), (1, 1))
SPOT = ((0, 96), (96, 96), (192, 48), (240, 48), (288, 16), (304, 16), (320, 16), (336, 16))
RIM = 352
BODY = 3 * PX
LATE = 3 * (MAIN + SIDE)


def opposite(side):
    dr, dc = SIDES[side]
    return SIDES.index((-dr, -dc))


def at1(frame, row, col):
    return (frame * ER1 + row) * EC + col


def at2(frame, row, col):
    return (frame * ER2 + row) * EC + col


def norm_act(low, high, gain_low, gain_high):
    total = jnp.sum(low * low + 0.5 * (high * high), axis=-1, keepdims=True)
    scale = lax.rsqrt(total * (1.0 / C) + 1e-06)

    def silu(values, gain):
        half = 0.5 * (values * scale * gain)
        return half + half * jnp.tanh(half)

    return silu(low, gain_low), silu(high, gain_high)


def twice(high):
    return jnp.concatenate([high, high], axis=-1)


def first_half(lines):
    return lax.broadcasted_iota(jnp.int32, (lines, LO), 1) < 64


def swap(value):
    return pltpu.roll(value, 64, 1)


def join(first, second):
    return jnp.where(first_half(first.shape[0]), first, second)


def split(value):
    mask, other = first_half(value.shape[0]), swap(value)
    return jnp.where(mask, value, other), jnp.where(mask, other, value)


def kernel(sizes, x_hbm, w1_hbm, w2_hbm, g1_hbm, g2_hbm, out,
           x, gains, wlo, whi, wti, elo1, ehi1, elo2, ehi2, taps1, sides1, taps2,
           body_s, body_r, rim_s, rim_r, late_s, late_r,
           load_sem, w_sem, rim_ss, rim_rs, z_ss, z_rs, ready):
    n_tm, n_row, n_col = sizes
    tm, row, col = (lax.axis_index(name) for name in ("tm", "row", "col"))
    scope = jax.named_scope

    def neighbour(dr, dc):
        return (tm, lax.rem(row + (dr + n_row), n_row), lax.rem(col + (dc + n_col), n_col))

    later = (lax.rem(tm + 1, n_tm), row, col)
    earlier = (lax.rem(tm + (n_tm - 1), n_tm), row, col)
    has_later = tm < n_tm - 1
    has_earlier = tm > 0

    barrier = pltpu.get_barrier_semaphore()
    for dr, dc in SIDES:
        pl.semaphore_signal(barrier, inc=1, device_id=neighbour(dr, dc), device_id_type=MESH)

    @pl.when(has_later)
    def _():
        pl.semaphore_signal(barrier, inc=1, device_id=later, device_id_type=MESH)

    loads = [pltpu.make_async_copy(x_hbm, x, load_sem.at[0])]
    for k, g in enumerate((g1_hbm, g2_hbm)):
        loads.append(pltpu.make_async_copy(g, gains.at[k], load_sem.at[k + 1]))
    for load in loads:
        load.start()
    w_loads = []
    for k, w in enumerate((w1_hbm, w2_hbm)):
        group = [
            pltpu.make_async_copy(w.at[:, :, :, 0:128, :], wlo.at[k], w_sem.at[k, 0]),
            pltpu.make_async_copy(w.at[:, :, 0:2, 128:192, :], whi.at[k], w_sem.at[k, 1]),
            pltpu.make_async_copy(w.at[:, :, 2, 128:192, :], wti.at[k, :, 0:3], w_sem.at[k, 2]),
        ]
        for load in group:
            load.start()
        w_loads.append(group)

    wti[:, :, 3] = jnp.zeros((2, 3, 64, C), BF)

    @pl.when(jnp.logical_not(has_earlier))
    def _():
        body_r[...] = jnp.zeros((BODY, LO), BF)
        rim_r[0] = jnp.zeros((RIM, LO), BF)
        late_r[...] = jnp.zeros((LATE, LO), BF)

    keep_row = {-1: jnp.where(row > 0, 1.0, 0.0), 1: jnp.where(row < n_row - 1, 1.0, 0.0)}
    keep_col = {-1: jnp.where(col > 0, 1.0, 0.0), 1: jnp.where(col < n_col - 1, 1.0, 0.0)}

    def side_keep(side):
        dr, dc = SIDES[side]
        if dr and dc:
            return keep_row[dr] * keep_col[dc]
        return keep_row[dr] if dr else keep_col[dc]

    def rim_copy(side):
        here, size = SPOT[side]
        there, _ = SPOT[opposite(side)]
        return pltpu.make_async_remote_copy(
            src_ref=rim_s.at[:, pl.ds(here, size)], dst_ref=rim_r.at[1:3, pl.ds(there, size)],
            send_sem=rim_ss.at[side], recv_sem=rim_rs.at[opposite(side)],
            device_id=neighbour(*SIDES[side]), device_id_type=MESH)

    def z_copy(k):
        src, dst = ((body_s, body_r), (rim_r.at[2], rim_r.at[0]), (late_s, late_r))[k]
        return pltpu.make_async_remote_copy(
            src_ref=src, dst_ref=dst, send_sem=z_ss.at[k], recv_sem=z_rs.at[k],
            device_id=later, device_id_type=MESH)

    def z_start(k):
        pl.when(has_later)(lambda: z_copy(k).start())

    def z_wait(k):
        pl.when(has_earlier)(lambda: z_copy(k).wait_recv())

    def put_body1(frame, low, high):
        for r in range(RO):
            elo1[pl.ds(at1(frame, r + 2, 8), CO)] = low[r * CO:(r + 1) * CO]
            ehi1[pl.ds(at1(frame, r + 2, 8), CO)] = high[r * CO:(r + 1) * CO]

    def pack_rims(pair):
        f = 2 + 2 * pair
        for side, (dr, dc) in enumerate(SIDES):
            spot, _ = SPOT[side]
            r = 2 if dr < 0 else RO
            c = 8 if dc < 0 else 22
            if dc == 0:
                for q in range(2):
                    for i in range(2):
                        to = spot + (2 * i + q) * CO
                        rim_s[pair, to:to + CO] = elo1[pl.ds(at1(f + i, r + q, 8), CO)].astype(BF)
                    high = join(*[ehi1[pl.ds(at1(f + i, r + q, 8), CO)] for i in range(2)])
                    to = spot + 64 + q * CO
                    rim_s[pair, to:to + CO] = high.astype(BF)
            elif dr == 0:
                for i in range(2):
                    low = [elo1[pl.ds(at1(f + i, 2, c + q), RO, stride=EC)] for q in range(2)]
                    to = spot + i * CO
                    rim_s[pair, to:to + CO] = jnp.concatenate(low, axis=0).astype(BF)
                high = [join(*[ehi1[pl.ds(at1(f + i, 2, c + q), RO, stride=EC)] for i in range(2)]) for q in range(2)]
                rim_s[pair, spot + 32:spot + 48] = jnp.concatenate(high, axis=0).astype(BF)
            else:
                pairs = lax.broadcasted_iota(jnp.int32, (8, LO), 0) // 2
                low = high = jnp.zeros((8, LO), F32)
                for i in range(2):
                    for q in range(2):
                        k = 2 * i + q
                        low = jnp.where(pairs == k, elo1[pl.ds(at1(f + i, r + q, c) - 2 * k, 8)], low)
                for q in range(2):
                    both = join(*[ehi1[pl.ds(at1(f + i, r + q, c) - 2 * q, 8)] for i in range(2)])
                    high = jnp.where(pairs == q, both, high)
                rim_s[pair, spot:spot + 16] = jnp.concatenate([low, high], axis=0).astype(BF)

    def put_rims(slot):
        f = 2 * slot
        for side, (dr, dc) in enumerate(SIDES):
            spot, size = SPOT[side]
            r = 0 if dr < 0 else RO + 2
            c = 6 if dc < 0 else 24
            value = rim_r[slot, spot:spot + size].astype(F32) * side_keep(side)
            if dc == 0:
                high = split(value[64:96])
                for i in range(2):
                    for q in range(2):
                        elo1[pl.ds(at1(f + i, r + q, 8), CO)] = value[(2 * i + q) * CO:(2 * i + q + 1) * CO]
                        ehi1[pl.ds(at1(f + i, r + q, 8), CO)] = high[i][q * CO:(q + 1) * CO]
            elif dr == 0:
                high = split(value[32:48])
                for i in range(2):
                    for q in range(2):
                        k = 2 * i + q
                        elo1[pl.ds(at1(f + i, 2, c + q), RO, stride=EC)] = value[k * RO:(k + 1) * RO]
                        ehi1[pl.ds(at1(f + i, 2, c + q), RO, stride=EC)] = high[i][q * RO:(q + 1) * RO]
            else:
                high = split(value[8:16])
                for i in range(2):
                    for q in range(2):
                        k = 2 * i + q
                        elo1[pl.ds(at1(f + i, r + q, c), 2)] = value[2 * k:2 * k + 2]
                        ehi1[pl.ds(at1(f + i, r + q, c), 2)] = high[i][2 * q:2 * q + 2]

    def lanes(low, high, below):
        wide = jnp.concatenate(low + [join(high[0], high[1])], axis=1).astype(BF)
        return wide, join(high[2], below).astype(BF)

    def build1(frame):
        for r in range(ER1):
            low = [elo1[pl.ds(at1(frame, r, 7 + c), CO)] for c in range(3)]
            high = [ehi1[pl.ds(at1(frame, r, 7 + c), CO)] for c in range(3)]
            below = ehi1[pl.ds(at1(frame, min(r + 1, ER1 - 1), 9), CO)]
            wide, tight = lanes(low, high, below)
            taps1[frame, r * CO:(r + 1) * CO, 0:512] = wide
            taps1[frame, r * CO:(r + 1) * CO, 512:640] = tight
        for s, c0 in enumerate((6, 23)):
            lines = slice(s * CO, (s + 1) * CO)
            for b in range(3):
                low = [elo1[pl.ds(at1(frame, b, c0 + c), CO, stride=EC)] for c in range(3)]
                high = [ehi1[pl.ds(at1(frame, b, c0 + c), CO, stride=EC)] for c in range(3)]
                below = high[2]
                if b == 0:
                    below = ehi1[pl.ds(at1(frame, 1, c0 + 2), CO, stride=EC)]
                wide, tight = lanes(low, high, below)
                sides1[frame, lines, b * 512:(b + 1) * 512] = wide
                if b != 1:
                    sides1[frame, lines, 1536 + b * 64:1664 + b * 64] = tight

    def build2(frame):
        for r in range(ER2):
            low = [elo2[pl.ds(at2(frame, r, 7 + c), CO)] for c in range(3)]
            high = [ehi2[pl.ds(at2(frame, r, 7 + c), CO)] for c in range(3)]
            below = ehi2[pl.ds(at2(frame, min(r + 1, ER2 - 1), 9), CO)]
            wide, tight = lanes(low, high, below)
            taps2[frame, r * CO:(r + 1) * CO, 0:512] = wide
            taps2[frame, r * CO:(r + 1) * CO, 512:640] = tight

    def conv(k, a, frame):
        f = frame - 2 + a
        taps, rows = ((taps1, ER2), (taps2, RO))[k]
        count = rows * CO
        left = [taps[f:f + 2, b * CO:b * CO + count, 0:512].reshape(2 * count, 512) for b in range(3)]
        left += [taps[f:f + 2, b * CO:b * CO + count, 512:640].reshape(2 * count, LO) for b in (0, 2)]
        left = jnp.concatenate(left, axis=1)
        if k == 0:
            left = jnp.concatenate([left, sides1[f:f + 2].reshape(2 * SIDE, 14 * LO)], axis=0)
        right = []
        for b in range(3):
            right += [wlo[k, a, b].reshape(3 * LO, C), whi[k, a, b].reshape(LO, C)]
        right.append(wti[k, a].reshape(2 * LO, C))
        return jnp.dot(left, jnp.concatenate(right, axis=0), preferred_element_type=F32)

    def put2(frame, low, high):
        for i in range(2):
            for r in range(ER2):
                lines = slice(i * MAIN + r * CO, i * MAIN + (r + 1) * CO)
                elo2[pl.ds(at2(frame + i, r, 8), CO)] = low[lines]
                ehi2[pl.ds(at2(frame + i, r, 8), CO)] = high[lines]
            for s, c in enumerate((7, 24)):
                here = 2 * MAIN + i * SIDE + s * CO
                for first, count in ((0, 8), (8, 2)):
                    lines = slice(here + first, here + first + count)
                    elo2[pl.ds(at2(frame + i, first, c), count, stride=EC)] = low[lines]
                    ehi2[pl.ds(at2(frame + i, first, c), count, stride=EC)] = high[lines]

    def inside(value):
        parts = []
        for i in range(2):
            here = i * MAIN
            parts.append(value[here:here + CO] * keep_row[-1])
            parts.append(value[here + CO:here + MAIN - CO])
            parts.append(value[here + MAIN - CO:here + MAIN] * keep_row[1])
        lines = lax.broadcasted_iota(jnp.int32, (CO, LO), 0)
        factor = jnp.where(lines == 0, keep_row[-1], jnp.where(lines == ER2 - 1, keep_row[1], 1.0))
        for i in range(2):
            for s, dc in enumerate((-1, 1)):
                here = 2 * MAIN + i * SIDE + s * CO
                parts.append(value[here:here + CO] * (factor * keep_col[dc]))
        return jnp.concatenate(parts, axis=0)

    def finish_first(total):
        low, high = norm_act(total[:, :LO], twice(total[:, LO:]), *gain[1])
        return inside(low), inside(high)

    def finish_second(frame, total):
        f = frame - 2
        total = total + x[f:f + 2].reshape(2 * PX, C).astype(F32)
        out[f:f + 2] = total.astype(BF).reshape(2, RO, CO, C)

    with scope("load"):
        for load in loads:
            load.wait()
        gain = []
        for k in range(2):
            value = gains[k]
            gain.append((value[:, :LO], twice(value[:, LO:])))
    with scope("norm"):
        kept = {}
        for f in (2, 3, 0, 1):
            value = x[f].reshape(PX, C).astype(F32)
            low, high = norm_act(value[:, :LO], twice(value[:, LO:]), *gain[0])
            put_body1(f + 2, low, high)
            kept[f] = low, high
        pack_rims(1)
        pack_rims(0)
        for i in range(2):
            body_s[i * PX:(i + 1) * PX] = kept[2 + i][0].astype(BF)
        body_s[2 * PX:3 * PX] = join(kept[2][1], kept[3][1]).astype(BF)

    with scope("barrier"):
        pl.semaphore_wait(barrier, jnp.where(has_earlier, 9, 8))

        @pl.when(has_earlier)
        def _():
            pl.semaphore_signal(ready, inc=1, device_id=earlier, device_id_type=MESH)
    with scope("send_rims"):
        for side in range(8):
            rim_copy(side).start()
    with scope("send_cache"):
        @pl.when(has_later)
        def _():
            pl.semaphore_wait(ready, 1)
            z_copy(0).start()

    with scope("wait_rims"):
        for side in range(8):
            rim_copy(opposite(side)).wait_recv()
        z_start(1)
    with scope("build_own"):
        put_rims(2)
        build1(4)
        build1(5)
        put_rims(1)
        build1(2)
        build1(3)
    with scope("wait_weights"):
        for load in w_loads[0]:
            load.wait()
    with scope("conv_first"):
        low, high = finish_first(conv(0, 0, 4) + conv(0, 1, 4) + conv(0, 2, 4))
        count = 2 * (MAIN + SIDE)
        late_s[0:count] = low.astype(BF)
        late_s[count:count + MAIN] = join(high[0:MAIN], high[MAIN:2 * MAIN]).astype(BF)
        late_s[count + MAIN:LATE] = join(high[2 * MAIN:2 * MAIN + SIDE], high[2 * MAIN + SIDE:]).astype(BF)
        z_start(2)
        put2(4, low, high)
        total = conv(0, 2, 2)

    with scope("wait_cache"):
        z_wait(0)
        z_wait(1)
    with scope("build_cache"):
        low, high = body_r[0:2 * PX].astype(F32), split(body_r[2 * PX:3 * PX].astype(F32))
        for i in range(2):
            put_body1(i, low[i * PX:(i + 1) * PX], high[i])
        put_rims(0)
        build1(0)
        build1(1)
    with scope("conv_first_early"):
        low, high = finish_first(total + conv(0, 1, 2) + conv(0, 0, 2))
        put2(2, low, high)

    with scope("build_second"):
        for f in (2, 3, 4, 5):
            build2(f)
    with scope("wait_weights"):
        for load in w_loads[1]:
            load.wait()
    with scope("conv_second"):
        finish_second(4, conv(1, 0, 4) + conv(1, 1, 4) + conv(1, 2, 4))
        total = conv(1, 2, 2)

    with scope("wait_late"):
        z_wait(2)
    with scope("build_late"):
        count = 2 * (MAIN + SIDE)
        low = late_r[0:count].astype(F32)
        main = split(late_r[count:count + MAIN].astype(F32))
        beside = split(late_r[count + MAIN:LATE].astype(F32))
        put2(0, low, jnp.concatenate([*main, *beside], axis=0))
        build2(0)
        build2(1)
    with scope("conv_late"):
        finish_second(2, total + conv(1, 1, 2) + conv(1, 0, 2))

    with scope("drain"):
        for side in range(8):
            rim_copy(side).wait_send()

        @pl.when(has_later)
        def _():
            for k in range(3):
                z_copy(k).wait_send()


def solution(mesh):
    sizes = tuple(mesh.shape[name] for name in ("tm", "row", "col"))

    def shards(features, conv_first, conv_second, gain_first, gain_second):
        in_hbm = pl.BlockSpec(memory_space=pltpu.HBM)
        dma = pltpu.SemaphoreType.DMA
        return pl.pallas_call(
            functools.partial(kernel, sizes),
            out_shape=pltpu.VMEM(features.shape, BF),
            in_specs=[in_hbm] * 5,
            out_specs=pl.BlockSpec(memory_space=pltpu.VMEM),
            scratch_shapes=[
                pltpu.VMEM((FR, RO, CO, C), BF),
                pltpu.VMEM((2, 1, C), F32),
                pltpu.VMEM((2, 3, 3, 3, LO, C), BF),
                pltpu.VMEM((2, 3, 3, 2, 64, C), BF),
                pltpu.VMEM((2, 3, 4, 64, C), BF),
                pltpu.VMEM(((EF + 1) * ER1 * EC, LO), F32),
                pltpu.VMEM(((EF + 1) * ER1 * EC, LO), F32),
                pltpu.VMEM((EF * ER2 * EC, LO), F32),
                pltpu.VMEM((EF * ER2 * EC, LO), F32),
                pltpu.VMEM((EF, ER1 * CO, 5 * LO), BF),
                pltpu.VMEM((EF, SIDE, 14 * LO), BF),
                pltpu.VMEM((EF, ER2 * CO, 5 * LO), BF),
                pltpu.VMEM((BODY, LO), BF),
                pltpu.VMEM((BODY, LO), BF),
                pltpu.VMEM((2, RIM, LO), BF),
                pltpu.VMEM((3, RIM, LO), BF),
                pltpu.VMEM((LATE, LO), BF),
                pltpu.VMEM((LATE, LO), BF),
                dma((3,)), dma((2, 3)), dma((8,)), dma((8,)), dma((3,)), dma((3,)), pltpu.SemaphoreType.REGULAR,
            ],
            compiler_params=pltpu.CompilerParams(
                collective_id=0, has_side_effects=True, vmem_limit_bytes=60 * 1024 * 1024),
        )(features, conv_first, conv_second, gain_first.reshape(1, C), gain_second.reshape(1, C))

    return jax.shard_map(
        shards, mesh=mesh, in_specs=(P("tm", "row", "col", None), P(), P(), P(), P()),
        out_specs=P("tm", "row", "col", None), check_vma=False)
```

```python
import functools

import jax
import jax.numpy as jnp
from jax import lax
from jax.experimental import pallas as pl
from jax.experimental.pallas import tpu as pltpu
from jax.sharding import PartitionSpec as P

MESH = pl.DeviceIdType.MESH
BF = jnp.bfloat16
F32 = jnp.float32
C = 192
LO = 128
FR, RO, CO = 4, 8, 16
PX = RO * CO
EF, ER1, ER2, EC = 6, 12, 10, 32
MAIN, SIDE = ER2 * CO, 2 * CO
EDGE = (6, 7, 8, 23, 24, 25)
EL = 32
SIDES = ((-1, 0), (1, 0), (0, -1), (0, 1), (-1, -1), (-1, 1), (1, -1), (1, 1))
SPOT = ((0, 96), (96, 96), (192, 48), (240, 48), (288, 16), (304, 16), (320, 16), (336, 16))
RIM = 352
BODY = 3 * PX
LINES = MAIN + SIDE
LATE = LINES * 3 // 2


def opposite(side):
    dr, dc = SIDES[side]
    return SIDES.index((-dr, -dc))


def at1(frame, row, col):
    return (frame * ER1 + row) * EC + col


def edge(frame, row, col):
    return (frame * len(EDGE) + EDGE.index(col)) * EL + row + 6


def at2(frame, row, col):
    return (frame * ER2 + row) * EC + col


def norm_act(low, high, gain_low, gain_high):
    total = jnp.sum(low * low + 0.5 * (high * high), axis=-1, keepdims=True)
    scale = lax.rsqrt(total * (1.0 / C) + 1e-06)

    def silu(values, gain):
        half = values * scale * gain
        return half + half * jnp.tanh(half)

    return silu(low, gain_low), silu(high, gain_high)


def twice(high):
    return jnp.concatenate([high, high], axis=-1)


def first_half(lines):
    return lax.broadcasted_iota(jnp.int32, (lines, LO), 1) < 64


def swap(value):
    return pltpu.roll(value, 64, 1)


def join(first, second):
    return jnp.where(first_half(first.shape[0]), first, second)


def split(value):
    mask, other = first_half(value.shape[0]), swap(value)
    return jnp.where(mask, value, other), jnp.where(mask, other, value)


def kernel(sizes, x_hbm, w1_hbm, w2_hbm, g1_hbm, g2_hbm, out,
           x, gains, wlo, whi, wti, elo1, ehi1, vlo, vhi, elo2, ehi2, taps1, sides1, taps2, sums1, sums2,
           body_s, body_r, rim_s, rim_r, late_s, late_r,
           load_sem, w_sem, rim_ss, rim_rs, z_ss, z_rs):
    n_tm, n_row, n_col = sizes
    tm, row, col = (lax.axis_index(name) for name in ("tm", "row", "col"))
    scope = jax.named_scope

    def neighbour(dr, dc):
        return (tm, lax.rem(row + (dr + n_row), n_row), lax.rem(col + (dc + n_col), n_col))

    later = (lax.rem(tm + 1, n_tm), row, col)
    earlier = (lax.rem(tm + (n_tm - 1), n_tm), row, col)
    has_later = tm < n_tm - 1
    has_earlier = tm > 0

    barrier = pltpu.get_barrier_semaphore()
    for dr, dc in SIDES:
        pl.semaphore_signal(barrier, inc=1, device_id=neighbour(dr, dc), device_id_type=MESH)

    @pl.when(has_earlier)
    def _():
        pl.semaphore_signal(barrier, inc=1, device_id=earlier, device_id_type=MESH)

    loads = [pltpu.make_async_copy(x_hbm, x, load_sem.at[0])]
    for k, g in enumerate((g1_hbm, g2_hbm)):
        loads.append(pltpu.make_async_copy(g, gains.at[k], load_sem.at[k + 1]))
    for load in loads:
        load.start()
    w_loads = []
    for k, w in enumerate((w1_hbm, w2_hbm)):
        group = [
            pltpu.make_async_copy(w.at[:, :, :, 0:128, :], wlo.at[k], w_sem.at[k, 0]),
            pltpu.make_async_copy(w.at[:, :, 0:2, 128:192, :], whi.at[k], w_sem.at[k, 1]),
            pltpu.make_async_copy(w.at[:, :, 2, 128:192, :], wti.at[k, :, 0:3], w_sem.at[k, 2]),
        ]
        for load in group:
            load.start()
        w_loads.append(group)

    wti[:, :, 3] = jnp.zeros((2, 3, 64, C), BF)

    @pl.when(jnp.logical_not(has_earlier))
    def _():
        body_r[...] = jnp.zeros((BODY, LO), BF)
        rim_r[0] = jnp.zeros((RIM, LO), BF)
        late_r[...] = jnp.zeros((2, LATE, LO), BF)

    keep_row = {-1: jnp.where(row > 0, 1.0, 0.0), 1: jnp.where(row < n_row - 1, 1.0, 0.0)}
    keep_col = {-1: jnp.where(col > 0, 1.0, 0.0), 1: jnp.where(col < n_col - 1, 1.0, 0.0)}

    def side_keep(side):
        dr, dc = SIDES[side]
        if dr and dc:
            return keep_row[dr] * keep_col[dc]
        return keep_row[dr] if dr else keep_col[dc]

    def rim_copy(side):
        here, size = SPOT[side]
        there, _ = SPOT[opposite(side)]
        return pltpu.make_async_remote_copy(
            src_ref=rim_s.at[:, pl.ds(here, size)], dst_ref=rim_r.at[1:3, pl.ds(there, size)],
            send_sem=rim_ss.at[side], recv_sem=rim_rs.at[opposite(side)],
            device_id=neighbour(*SIDES[side]), device_id_type=MESH)

    def z_copy(k):
        src, dst = (
            (body_s, body_r), (rim_r.at[2], rim_r.at[0]),
            (late_s.at[0], late_r.at[0]), (late_s.at[1], late_r.at[1]))[k]
        return pltpu.make_async_remote_copy(
            src_ref=src, dst_ref=dst, send_sem=z_ss.at[k], recv_sem=z_rs.at[k],
            device_id=later, device_id_type=MESH)

    def z_start(k):
        pl.when(has_later)(lambda: z_copy(k).start())

    def z_wait(k):
        pl.when(has_earlier)(lambda: z_copy(k).wait_recv())

    def put_body1(frame, low, high):
        for r in range(RO):
            elo1[pl.ds(at1(frame, r + 2, 8), CO)] = low[r * CO:(r + 1) * CO]
            ehi1[pl.ds(at1(frame, r + 2, 8), CO)] = high[r * CO:(r + 1) * CO]

    def pack_rims(pair):
        f = 2 + 2 * pair
        for side, (dr, dc) in enumerate(SIDES):
            spot, _ = SPOT[side]
            r = 2 if dr < 0 else RO
            c = 8 if dc < 0 else 22
            if dc == 0:
                for q in range(2):
                    for i in range(2):
                        to = spot + (2 * i + q) * CO
                        rim_s[pair, to:to + CO] = elo1[pl.ds(at1(f + i, r + q, 8), CO)].astype(BF)
                    high = join(*[ehi1[pl.ds(at1(f + i, r + q, 8), CO)] for i in range(2)])
                    to = spot + 64 + q * CO
                    rim_s[pair, to:to + CO] = high.astype(BF)
            elif dr == 0:
                outer = 0 if dc < 0 else 1
                high = []
                for i in range(2):
                    low = [elo1[pl.ds(at1(f + i, 2, c + q), RO, stride=EC)] for q in range(2)]
                    high.append([ehi1[pl.ds(at1(f + i, 2, c + q), RO, stride=EC)] for q in range(2)])
                    to = spot + i * CO
                    rim_s[pair, to:to + CO] = jnp.concatenate(low, axis=0).astype(BF)
                    vlo[pl.ds(edge(f + i, 2, c + outer), RO)] = low[outer]
                    vhi[pl.ds(edge(f + i, 2, c + outer), RO)] = high[i][outer]
                both = [join(high[0][q], high[1][q]) for q in range(2)]
                rim_s[pair, spot + 32:spot + 48] = jnp.concatenate(both, axis=0).astype(BF)
            else:
                pairs = lax.broadcasted_iota(jnp.int32, (8, LO), 0) // 2
                low = high = jnp.zeros((8, LO), F32)
                for i in range(2):
                    for q in range(2):
                        k = 2 * i + q
                        low = jnp.where(pairs == k, elo1[pl.ds(at1(f + i, r + q, c) - 2 * k, 8)], low)
                for q in range(2):
                    both = join(*[ehi1[pl.ds(at1(f + i, r + q, c) - 2 * q, 8)] for i in range(2)])
                    high = jnp.where(pairs == q, both, high)
                rim_s[pair, spot:spot + 16] = jnp.concatenate([low, high], axis=0).astype(BF)

    def put_rims(slot):
        f = 2 * slot
        for side, (dr, dc) in enumerate(SIDES):
            spot, size = SPOT[side]
            r = 0 if dr < 0 else RO + 2
            c = 6 if dc < 0 else 24
            value = rim_r[slot, spot:spot + size].astype(F32) * side_keep(side)
            near = 1 if dc < 0 else 0
            for i in range(2):
                for q in range(2):
                    k = 2 * i + q
                    if dc == 0:
                        low, high = value[k * CO:(k + 1) * CO], split(value[64:96])[i][q * CO:(q + 1) * CO]
                        elo1[pl.ds(at1(f + i, r + q, 8), CO)] = low
                        ehi1[pl.ds(at1(f + i, r + q, 8), CO)] = high
                        for line, border in ((0, 8), (CO - 1, 23)):
                            vlo[pl.ds(edge(f + i, r + q, border), 1)] = low[line:line + 1]
                            vhi[pl.ds(edge(f + i, r + q, border), 1)] = high[line:line + 1]
                    elif dr == 0:
                        low, high = value[k * RO:(k + 1) * RO], split(value[32:48])[i][q * RO:(q + 1) * RO]
                        vlo[pl.ds(edge(f + i, 2, c + q), RO)] = low
                        vhi[pl.ds(edge(f + i, 2, c + q), RO)] = high
                        if q == near:
                            elo1[pl.ds(at1(f + i, 2, c + q), RO, stride=EC)] = low
                            ehi1[pl.ds(at1(f + i, 2, c + q), RO, stride=EC)] = high
                    else:
                        low, high = value[2 * k:2 * k + 2], split(value[8:16])[i][2 * q:2 * q + 2]
                        for j in range(2):
                            vlo[pl.ds(edge(f + i, r + q, c + j), 1)] = low[j:j + 1]
                            vhi[pl.ds(edge(f + i, r + q, c + j), 1)] = high[j:j + 1]
                        elo1[pl.ds(at1(f + i, r + q, c + near), 1)] = low[near:near + 1]
                        ehi1[pl.ds(at1(f + i, r + q, c + near), 1)] = high[near:near + 1]

    def lanes(low, high, below):
        wide = jnp.concatenate(low + [join(high[0], high[1])], axis=1).astype(BF)
        return wide, join(high[2], below).astype(BF)

    def build(elo, ehi, at, rows, taps, frame):
        last = ehi[pl.ds(at(frame, rows - 1, 9), CO)]
        for r in reversed(range(rows)):
            low = [elo[pl.ds(at(frame, r, 7 + c), CO)] for c in range(3)]
            high = [ehi[pl.ds(at(frame, r, 7 + c), CO)] for c in range(2)]
            high.append(last if r == rows - 1 else ehi[pl.ds(at(frame, r, 9), CO)])
            wide, tight = lanes(low, high, last)
            last = high[2]
            taps[frame, r * CO:(r + 1) * CO, 0:512] = wide
            taps[frame, r * CO:(r + 1) * CO, 512:640] = tight

    def build1(frame):
        build(elo1, ehi1, at1, ER1, taps1, frame)
        for s in range(2):
            lines = slice(s * CO, (s + 1) * CO)
            cols = EDGE[3 * s:3 * s + 3]
            low = [[vlo[pl.ds(edge(frame, b, c), CO)] for c in cols] for b in range(3)]
            high = [[vhi[pl.ds(edge(frame, b, c), CO)] for c in cols] for b in range(3)]
            for b in range(3):
                wide, tight = lanes(low[b], high[b], high[min(b + 1, 2)][2])
                sides1[frame, lines, b * 512:(b + 1) * 512] = wide
                if b != 1:
                    sides1[frame, lines, 1536 + b * 64:1664 + b * 64] = tight

    def build2(frame):
        build(elo2, ehi2, at2, ER2, taps2, frame)

    def conv(k, jobs, halves=False):
        taps, count, sums = ((taps1, MAIN, sums1), (taps2, PX, sums2))[k]
        for target, a in jobs:
            f = target - 2 + a
            left = [taps[f, b * CO:b * CO + count, 0:512] for b in range(3)]
            left += [taps[f, b * CO:b * CO + count, 512:640] for b in (0, 2)]
            left = jnp.concatenate(left, axis=1)
            if k == 0:
                left = jnp.concatenate([left, sides1[f]], axis=0)
            right = []
            for b in range(3):
                right += [wlo[k, a, b].reshape(3 * LO, C), whi[k, a, b].reshape(LO, C)]
            right = jnp.concatenate(right + [wti[k, a].reshape(2 * LO, C)], axis=0)
            size = left.shape[0] // 2 if halves else left.shape[0]
            for here in range(0, left.shape[0], size):
                part = jnp.dot(left[here:here + size], right, preferred_element_type=F32)
                if (k, target) in begun:
                    part = part + sums[target - 2, here:here + size]
                sums[target - 2, here:here + size] = part
            begun.add((k, target))

    begun = set()

    def put2(frame, low, high):
        for r in range(ER2):
            lines = slice(r * CO, (r + 1) * CO)
            elo2[pl.ds(at2(frame, r, 8), CO)] = low[lines]
            ehi2[pl.ds(at2(frame, r, 8), CO)] = high[lines]
        for s, c in enumerate((7, 24)):
            for first, count in ((0, 8), (8, 2)):
                lines = slice(MAIN + s * CO + first, MAIN + s * CO + first + count)
                elo2[pl.ds(at2(frame, first, c), count, stride=EC)] = low[lines]
                ehi2[pl.ds(at2(frame, first, c), count, stride=EC)] = high[lines]

    def inside(value):
        parts = [value[0:CO] * keep_row[-1], value[CO:MAIN - CO], value[MAIN - CO:MAIN] * keep_row[1]]
        lines = lax.broadcasted_iota(jnp.int32, (CO, LO), 0)
        factor = jnp.where(lines == 0, keep_row[-1], jnp.where(lines == ER2 - 1, keep_row[1], 1.0))
        for s, dc in enumerate((-1, 1)):
            parts.append(value[MAIN + s * CO:MAIN + (s + 1) * CO] * (factor * keep_col[dc]))
        return jnp.concatenate(parts, axis=0)

    def finish_first(frame):
        total = sums1[frame - 2]
        low, high = norm_act(total[:, :LO], twice(total[:, LO:]), *gain[1])
        return inside(low), inside(high)

    def finish_second(frame):
        f = frame - 2
        total = sums2[f] + x[f].reshape(PX, C).astype(F32)
        out[f] = total.astype(BF).reshape(RO, CO, C)

    def pack_late(i, low, high):
        late_s[i, 0:LINES] = low.astype(BF)
        late_s[i, LINES:LINES + 80] = join(high[0:80], high[80:160]).astype(BF)
        late_s[i, LINES + 80:LATE] = join(high[160:176], high[176:192]).astype(BF)

    def put_late(i):
        low = late_r[i, 0:LINES].astype(F32)
        main = split(late_r[i, LINES:LINES + 80].astype(F32))
        beside = split(late_r[i, LINES + 80:LATE].astype(F32))
        put2(i, low, jnp.concatenate([*main, *beside], axis=0))

    with scope("load"):
        for load in loads:
            load.wait()
        gain = []
        for k in range(2):
            value = 0.5 * gains[k]
            gain.append((value[:, :LO], twice(value[:, LO:])))
    with scope("norm"):
        kept = {}
        for f in (2, 3, 0, 1):
            value = x[f].reshape(PX, C).astype(F32)
            low, high = norm_act(value[:, :LO], twice(value[:, LO:]), *gain[0])
            put_body1(f + 2, low, high)
            kept[f] = low, high
        pack_rims(1)
        pack_rims(0)
        for i in range(2):
            body_s[i * PX:(i + 1) * PX] = kept[2 + i][0].astype(BF)
        body_s[2 * PX:3 * PX] = join(kept[2][1], kept[3][1]).astype(BF)

    with scope("barrier"):
        pl.semaphore_wait(barrier, jnp.where(has_later, 9, 8))
    with scope("send_rims"):
        for side in reversed(range(8)):
            rim_copy(side).start()
    with scope("send_cache"):
        z_start(0)

    with scope("wait_rims"):
        for side in range(8):
            rim_copy(opposite(side)).wait_recv()
        z_start(1)
    with scope("build_own"):
        put_rims(2)
        build1(4)
        build1(5)
        put_rims(1)
        build1(2)
        build1(3)
    with scope("wait_weights"):
        for load in w_loads[0]:
            load.wait()
    with scope("conv_first"):
        conv(0, ((5, 0), (4, 0), (5, 1), (4, 1), (5, 2), (4, 2)))
        kept = {}
        for f in (5, 4):
            kept[f] = finish_first(f)
            pack_late(f - 4, *kept[f])
    with scope("send_late"):
        z_start(3)
        z_start(2)
    with scope("conv_ahead"):
        conv(0, ((2, 2), (3, 2)))
        conv(0, ((3, 1),), halves=True)
        for f in (4, 5):
            put2(f, *kept[f])
            build2(f)
        for load in w_loads[1]:
            load.wait()
        conv(1, ((4, 2), (5, 2)))
        conv(1, ((5, 1),), halves=True)

    with scope("wait_cache"):
        z_wait(0)
        z_wait(1)
    with scope("build_cache"):
        low, high = body_r[0:2 * PX].astype(F32), split(body_r[2 * PX:3 * PX].astype(F32))
        for i in range(2):
            put_body1(i, low[i * PX:(i + 1) * PX], high[i])
            for border in (8, 23):
                vlo[pl.ds(edge(i, 2, border), RO)] = elo1[pl.ds(at1(i, 2, border), RO, stride=EC)]
                vhi[pl.ds(edge(i, 2, border), RO)] = ehi1[pl.ds(at1(i, 2, border), RO, stride=EC)]
        put_rims(0)
        build1(0)
        build1(1)
    with scope("conv_first_early"):
        conv(0, ((2, 0), (3, 0)))
        conv(0, ((2, 1),), halves=True)
        for f in (2, 3):
            put2(f, *finish_first(f))
            build2(f)
    with scope("conv_second"):
        conv(1, ((4, 0), (5, 0), (4, 1), (3, 1), (2, 2), (3, 2)))
        finish_second(4)
        finish_second(5)

    with scope("wait_late"):
        z_wait(3)
    with scope("conv_late"):
        put_late(1)
        build2(1)
        conv(1, ((3, 0), (2, 1)))
        finish_second(3)
    with scope("wait_last"):
        z_wait(2)
    with scope("conv_last"):
        put_late(0)
        build2(0)
        conv(1, ((2, 0),), halves=True)
        finish_second(2)

    with scope("drain"):
        for side in range(8):
            rim_copy(side).wait_send()

        @pl.when(has_later)
        def _():
            for k in range(4):
                z_copy(k).wait_send()


def solution(mesh):
    sizes = tuple(mesh.shape[name] for name in ("tm", "row", "col"))

    def shards(features, conv_first, conv_second, gain_first, gain_second):
        in_hbm = pl.BlockSpec(memory_space=pltpu.HBM)
        dma = pltpu.SemaphoreType.DMA
        return pl.pallas_call(
            functools.partial(kernel, sizes),
            out_shape=pltpu.VMEM(features.shape, BF),
            in_specs=[in_hbm] * 5,
            out_specs=pl.BlockSpec(memory_space=pltpu.VMEM),
            scratch_shapes=[
                pltpu.VMEM((FR, RO, CO, C), BF),
                pltpu.VMEM((2, 1, C), F32),
                pltpu.VMEM((2, 3, 3, 3, LO, C), BF),
                pltpu.VMEM((2, 3, 3, 2, 64, C), BF),
                pltpu.VMEM((2, 3, 4, 64, C), BF),
                pltpu.VMEM((EF * ER1 * EC, LO), F32),
                pltpu.VMEM((EF * ER1 * EC, LO), F32),
                pltpu.VMEM((EF * len(EDGE) * EL, LO), F32),
                pltpu.VMEM((EF * len(EDGE) * EL, LO), F32),
                pltpu.VMEM((EF * ER2 * EC, LO), F32),
                pltpu.VMEM((EF * ER2 * EC, LO), F32),
                pltpu.VMEM((EF, ER1 * CO, 5 * LO), BF),
                pltpu.VMEM((EF, SIDE, 14 * LO), BF),
                pltpu.VMEM((EF, ER2 * CO, 5 * LO), BF),
                pltpu.VMEM((FR, MAIN + SIDE, C), F32),
                pltpu.VMEM((FR, PX, C), F32),
                pltpu.VMEM((BODY, LO), BF),
                pltpu.VMEM((BODY, LO), BF),
                pltpu.VMEM((2, RIM, LO), BF),
                pltpu.VMEM((3, RIM, LO), BF),
                pltpu.VMEM((2, LATE, LO), BF),
                pltpu.VMEM((2, LATE, LO), BF),
                dma((3,)), dma((2, 3)), dma((8,)), dma((8,)), dma((4,)), dma((4,)),
            ],
            compiler_params=pltpu.CompilerParams(
                collective_id=0, has_side_effects=True, vmem_limit_bytes=60 * 1024 * 1024),
        )(features, conv_first, conv_second, gain_first.reshape(1, C), gain_second.reshape(1, C))

    return jax.shard_map(
        shards, mesh=mesh, in_specs=(P("tm", "row", "col", None), P(), P(), P(), P()),
        out_specs=P("tm", "row", "col", None), check_vma=False)
```

```python
import functools

import jax
import jax.numpy as jnp
from jax import lax
from jax.experimental import pallas as pl
from jax.experimental.pallas import tpu as pltpu
from jax.sharding import PartitionSpec as P

MESH = pl.DeviceIdType.MESH
BF = jnp.bfloat16
F32 = jnp.float32
C = 192
LO = 128
FR, RO, CO = 4, 8, 16
PX = RO * CO
EF, ER1, ER2, EC = 6, 12, 10, 32
MAIN, SIDE = ER2 * CO, 2 * CO
EDGE = (6, 7, 8, 23, 24, 25)
EL = 32
SIDES = ((-1, 0), (1, 0), (0, -1), (0, 1), (-1, -1), (-1, 1), (1, -1), (1, 1))
SPOT = ((0, 96), (96, 96), (192, 48), (240, 48), (288, 16), (304, 16), (320, 16), (336, 16))
RIM = 352
BODY = 3 * PX


def opposite(side):
    dr, dc = SIDES[side]
    return SIDES.index((-dr, -dc))


def at1(frame, row, col):
    return (frame * ER1 + row) * EC + col


def edge(frame, row, col):
    return (frame * len(EDGE) + EDGE.index(col)) * EL + row + 6


def at2(frame, row, col):
    return (frame * ER2 + row) * EC + col


def norm_act(low, high, gain_low, gain_high):
    total = jnp.sum(low * low + 0.5 * (high * high), axis=-1, keepdims=True)
    scale = lax.rsqrt(total * (1.0 / C) + 1e-06)

    def silu(values, gain):
        half = values * scale * gain
        return half + half * jnp.tanh(half)

    return silu(low, gain_low), silu(high, gain_high)


def twice(high):
    return jnp.concatenate([high, high], axis=-1)


def first_half(lines):
    return lax.broadcasted_iota(jnp.int32, (lines, LO), 1) < 64


def swap(value):
    return pltpu.roll(value, 64, 1)


def join(first, second):
    return jnp.where(first_half(first.shape[0]), first, second)


def split(value):
    mask, other = first_half(value.shape[0]), swap(value)
    return jnp.where(mask, value, other), jnp.where(mask, other, value)


def kernel(sizes, x_hbm, w1_hbm, w2_hbm, g1_hbm, g2_hbm, out,
           x, gains, wlo, whi, wti, elo1, ehi1, vlo, vhi, elo2, ehi2, taps1, sides1, taps2, sums1, sums2,
           body_s, body_r, rim_s, rim_r, late_s, late_r,
           load_sem, w_sem, rim_ss, rim_rs, z_ss, z_rs):
    n_tm, n_row, n_col = sizes
    tm, row, col = (lax.axis_index(name) for name in ("tm", "row", "col"))
    scope = jax.named_scope

    def neighbour(dr, dc):
        return (tm, lax.rem(row + (dr + n_row), n_row), lax.rem(col + (dc + n_col), n_col))

    later = (lax.rem(tm + 1, n_tm), row, col)
    earlier = (lax.rem(tm + (n_tm - 1), n_tm), row, col)
    has_later = tm < n_tm - 1
    has_earlier = tm > 0

    barrier = pltpu.get_barrier_semaphore()
    for dr, dc in SIDES:
        pl.semaphore_signal(barrier, inc=1, device_id=neighbour(dr, dc), device_id_type=MESH)

    @pl.when(has_earlier)
    def _():
        pl.semaphore_signal(barrier, inc=1, device_id=earlier, device_id_type=MESH)

    loads = [pltpu.make_async_copy(x_hbm, x, load_sem.at[0])]
    for k, g in enumerate((g1_hbm, g2_hbm)):
        loads.append(pltpu.make_async_copy(g, gains.at[k], load_sem.at[k + 1]))
    for load in loads:
        load.start()
    w_loads = []
    for k, w in enumerate((w1_hbm, w2_hbm)):
        group = [
            pltpu.make_async_copy(w.at[:, :, :, 0:128, :], wlo.at[k], w_sem.at[k, 0]),
            pltpu.make_async_copy(w.at[:, :, 0:2, 128:192, :], whi.at[k], w_sem.at[k, 1]),
            pltpu.make_async_copy(w.at[:, :, 2, 128:192, :], wti.at[k, :, 0:3], w_sem.at[k, 2]),
        ]
        for load in group:
            load.start()
        w_loads.append(group)

    wti[:, :, 3] = jnp.zeros((2, 3, 64, C), BF)

    @pl.when(jnp.logical_not(has_earlier))
    def _():
        late_r[...] = jnp.zeros((BODY, LO), BF)

    keep_row = {-1: jnp.where(row > 0, 1.0, 0.0), 1: jnp.where(row < n_row - 1, 1.0, 0.0)}
    keep_col = {-1: jnp.where(col > 0, 1.0, 0.0), 1: jnp.where(col < n_col - 1, 1.0, 0.0)}

    def side_keep(side):
        dr, dc = SIDES[side]
        if dr and dc:
            return keep_row[dr] * keep_col[dc]
        return keep_row[dr] if dr else keep_col[dc]

    def rim_copy(side):
        here, size = SPOT[side]
        there, _ = SPOT[opposite(side)]
        return pltpu.make_async_remote_copy(
            src_ref=rim_s.at[:, pl.ds(here, size)], dst_ref=rim_r.at[1:3, pl.ds(there, size)],
            send_sem=rim_ss.at[side], recv_sem=rim_rs.at[opposite(side)],
            device_id=neighbour(*SIDES[side]), device_id_type=MESH)

    def z_copy(k):
        src, dst = ((body_s, body_r), (rim_r.at[2], rim_r.at[0]), (late_s, late_r))[k]
        return pltpu.make_async_remote_copy(
            src_ref=src, dst_ref=dst, send_sem=z_ss.at[k], recv_sem=z_rs.at[k],
            device_id=later, device_id_type=MESH)

    def z_start(k):
        pl.when(has_later)(lambda: z_copy(k).start())

    def z_wait(k):
        pl.when(has_earlier)(lambda: z_copy(k).wait_recv())

    def put_body1(frame, low, high):
        for r in range(RO):
            elo1[pl.ds(at1(frame, r + 2, 8), CO)] = low[r * CO:(r + 1) * CO]
            ehi1[pl.ds(at1(frame, r + 2, 8), CO)] = high[r * CO:(r + 1) * CO]

    def pack_rims(pair):
        f = 2 + 2 * pair
        for side, (dr, dc) in enumerate(SIDES):
            spot, _ = SPOT[side]
            r = 2 if dr < 0 else RO
            c = 8 if dc < 0 else 22
            if dc == 0:
                for q in range(2):
                    for i in range(2):
                        to = spot + (2 * i + q) * CO
                        rim_s[pair, to:to + CO] = elo1[pl.ds(at1(f + i, r + q, 8), CO)].astype(BF)
                    high = join(*[ehi1[pl.ds(at1(f + i, r + q, 8), CO)] for i in range(2)])
                    to = spot + 64 + q * CO
                    rim_s[pair, to:to + CO] = high.astype(BF)
            elif dr == 0:
                outer = 0 if dc < 0 else 1
                high = []
                for i in range(2):
                    low = [elo1[pl.ds(at1(f + i, 2, c + q), RO, stride=EC)] for q in range(2)]
                    high.append([ehi1[pl.ds(at1(f + i, 2, c + q), RO, stride=EC)] for q in range(2)])
                    to = spot + i * CO
                    rim_s[pair, to:to + CO] = jnp.concatenate(low, axis=0).astype(BF)
                    vlo[pl.ds(edge(f + i, 2, c + outer), RO)] = low[outer]
                    vhi[pl.ds(edge(f + i, 2, c + outer), RO)] = high[i][outer]
                both = [join(high[0][q], high[1][q]) for q in range(2)]
                rim_s[pair, spot + 32:spot + 48] = jnp.concatenate(both, axis=0).astype(BF)
            else:
                pairs = lax.broadcasted_iota(jnp.int32, (8, LO), 0) // 2
                low = high = jnp.zeros((8, LO), F32)
                for i in range(2):
                    for q in range(2):
                        k = 2 * i + q
                        low = jnp.where(pairs == k, elo1[pl.ds(at1(f + i, r + q, c) - 2 * k, 8)], low)
                for q in range(2):
                    both = join(*[ehi1[pl.ds(at1(f + i, r + q, c) - 2 * q, 8)] for i in range(2)])
                    high = jnp.where(pairs == q, both, high)
                rim_s[pair, spot:spot + 16] = jnp.concatenate([low, high], axis=0).astype(BF)

    def put_rims(slot):
        f = 2 * slot
        for side, (dr, dc) in enumerate(SIDES):
            spot, size = SPOT[side]
            r = 0 if dr < 0 else RO + 2
            c = 6 if dc < 0 else 24
            value = rim_r[slot, spot:spot + size].astype(F32) * side_keep(side)
            near = 1 if dc < 0 else 0
            for i in range(2):
                for q in range(2):
                    k = 2 * i + q
                    if dc == 0:
                        low, high = value[k * CO:(k + 1) * CO], split(value[64:96])[i][q * CO:(q + 1) * CO]
                        elo1[pl.ds(at1(f + i, r + q, 8), CO)] = low
                        ehi1[pl.ds(at1(f + i, r + q, 8), CO)] = high
                        for line, border in ((0, 8), (CO - 1, 23)):
                            vlo[pl.ds(edge(f + i, r + q, border), 1)] = low[line:line + 1]
                            vhi[pl.ds(edge(f + i, r + q, border), 1)] = high[line:line + 1]
                    elif dr == 0:
                        low, high = value[k * RO:(k + 1) * RO], split(value[32:48])[i][q * RO:(q + 1) * RO]
                        vlo[pl.ds(edge(f + i, 2, c + q), RO)] = low
                        vhi[pl.ds(edge(f + i, 2, c + q), RO)] = high
                        if q == near:
                            elo1[pl.ds(at1(f + i, 2, c + q), RO, stride=EC)] = low
                            ehi1[pl.ds(at1(f + i, 2, c + q), RO, stride=EC)] = high
                    else:
                        low, high = value[2 * k:2 * k + 2], split(value[8:16])[i][2 * q:2 * q + 2]
                        for j in range(2):
                            vlo[pl.ds(edge(f + i, r + q, c + j), 1)] = low[j:j + 1]
                            vhi[pl.ds(edge(f + i, r + q, c + j), 1)] = high[j:j + 1]
                        elo1[pl.ds(at1(f + i, r + q, c + near), 1)] = low[near:near + 1]
                        ehi1[pl.ds(at1(f + i, r + q, c + near), 1)] = high[near:near + 1]

    def lanes(low, high, below):
        wide = jnp.concatenate(low + [join(high[0], high[1])], axis=1).astype(BF)
        return wide, join(high[2], below).astype(BF)

    def build(elo, ehi, at, rows, taps, frame):
        last = ehi[pl.ds(at(frame, rows - 1, 9), CO)]
        for r in reversed(range(rows)):
            low = [elo[pl.ds(at(frame, r, 7 + c), CO)] for c in range(3)]
            high = [ehi[pl.ds(at(frame, r, 7 + c), CO)] for c in range(2)]
            high.append(last if r == rows - 1 else ehi[pl.ds(at(frame, r, 9), CO)])
            wide, tight = lanes(low, high, last)
            last = high[2]
            taps[frame, r * CO:(r + 1) * CO, 0:512] = wide
            taps[frame, r * CO:(r + 1) * CO, 512:640] = tight

    def build1(frame):
        build(elo1, ehi1, at1, ER1, taps1, frame)
        for s in range(2):
            lines = slice(s * CO, (s + 1) * CO)
            cols = EDGE[3 * s:3 * s + 3]
            low = [[vlo[pl.ds(edge(frame, b, c), CO)] for c in cols] for b in range(3)]
            high = [[vhi[pl.ds(edge(frame, b, c), CO)] for c in cols] for b in range(3)]
            for b in range(3):
                wide, tight = lanes(low[b], high[b], high[min(b + 1, 2)][2])
                sides1[frame, lines, b * 512:(b + 1) * 512] = wide
                if b != 1:
                    sides1[frame, lines, 1536 + b * 64:1664 + b * 64] = tight

    def build2(frame):
        build(elo2, ehi2, at2, ER2, taps2, frame)

    def products(k, a, frames, pieces=1):
        taps, count = ((taps1, MAIN), (taps2, PX))[k]
        left = []
        for f in frames:
            parts = [taps[f, b * CO:b * CO + count, 0:512] for b in range(3)]
            parts += [taps[f, b * CO:b * CO + count, 512:640] for b in (0, 2)]
            left.append(jnp.concatenate(parts, axis=1))
            if k == 0:
                left.append(sides1[f])
        left = jnp.concatenate(left, axis=0)
        right = []
        for b in range(3):
            right += [wlo[k, a, b].reshape(3 * LO, C), whi[k, a, b].reshape(LO, C)]
        right = jnp.concatenate(right + [wti[k, a].reshape(2 * LO, C)], axis=0)
        size = left.shape[0] // (len(frames) * pieces)
        dots = len(frames) if pieces == 1 else pieces
        rows = left.shape[0] // (1 if pieces == 1 else pieces)
        made = [jnp.dot(left[i:i + rows], right, preferred_element_type=F32) for i in range(0, left.shape[0], rows)]
        if pieces > 1:
            return [(i * size, value) for i, value in enumerate(made)]
        return [made[0][i * size:(i + 1) * size] for i in range(dots)]

    def conv(k, a, targets, halves=False):
        sums = (sums1, sums2)[k]
        frames = [target - 2 + a for target in targets]
        if halves:
            parts = [(targets[0], here, value) for here, value in products(k, a, frames, 2)]
        else:
            parts = [(target, 0, value) for target, value in zip(targets, products(k, a, frames))]
        for target, here, part in parts:
            lines = slice(here, here + part.shape[0])
            if (k, target) in begun:
                part = part + sums[target - 2, lines]
            sums[target - 2, lines] = part
        begun.update((k, target) for target in targets)

    begun = set()

    def put2(frame, low, high):
        for r in range(ER2):
            lines = slice(r * CO, (r + 1) * CO)
            elo2[pl.ds(at2(frame, r, 8), CO)] = low[lines]
            ehi2[pl.ds(at2(frame, r, 8), CO)] = high[lines]
        for s, c in enumerate((7, 24)):
            for first, count in ((0, 8), (8, 2)):
                lines = slice(MAIN + s * CO + first, MAIN + s * CO + first + count)
                elo2[pl.ds(at2(frame, first, c), count, stride=EC)] = low[lines]
                ehi2[pl.ds(at2(frame, first, c), count, stride=EC)] = high[lines]

    def inside(value):
        parts = [value[0:CO] * keep_row[-1], value[CO:MAIN - CO], value[MAIN - CO:MAIN] * keep_row[1]]
        lines = lax.broadcasted_iota(jnp.int32, (CO, LO), 0)
        factor = jnp.where(lines == 0, keep_row[-1], jnp.where(lines == ER2 - 1, keep_row[1], 1.0))
        for s, dc in enumerate((-1, 1)):
            parts.append(value[MAIN + s * CO:MAIN + (s + 1) * CO] * (factor * keep_col[dc]))
        return jnp.concatenate(parts, axis=0)

    def finish_first(frame):
        total = sums1[frame - 2]
        low, high = norm_act(total[:, :LO], twice(total[:, LO:]), *gain[1])
        return inside(low), inside(high)

    def finish_second(frame):
        f = frame - 2
        total = sums2[f] + x[f].reshape(PX, C).astype(F32)
        if f < 2:
            low = late_r[f * PX:(f + 1) * PX].astype(F32)
            high = late_r[2 * PX:3 * PX].astype(F32)[:, f * 64:(f + 1) * 64]
            total = total + jnp.concatenate([low, high], axis=1)
        out[f] = total.astype(BF).reshape(RO, CO, C)

    def pack_late():
        last, first = products(1, 1, (5,))[0], products(1, 0, (4, 5))
        shares = [first[0] + last, first[1]]
        for i in range(2):
            late_s[i * PX:(i + 1) * PX] = shares[i][:, :LO].astype(BF)
        late_s[2 * PX:3 * PX] = jnp.concatenate([share[:, LO:] for share in shares], axis=1).astype(BF)

    with scope("load"):
        for load in loads:
            load.wait()
        gain = []
        for k in range(2):
            value = 0.5 * gains[k]
            gain.append((value[:, :LO], twice(value[:, LO:])))
    with scope("norm"):
        kept = {}
        for f in (2, 3, 0, 1):
            value = x[f].reshape(PX, C).astype(F32)
            low, high = norm_act(value[:, :LO], twice(value[:, LO:]), *gain[0])
            put_body1(f + 2, low, high)
            kept[f] = low, high
        pack_rims(1)
        pack_rims(0)
        for i in range(2):
            body_s[i * PX:(i + 1) * PX] = kept[2 + i][0].astype(BF)
        body_s[2 * PX:3 * PX] = join(kept[2][1], kept[3][1]).astype(BF)

    with scope("barrier"):
        pl.semaphore_wait(barrier, jnp.where(has_later, 9, 8))
    with scope("send_rims"):
        for side in reversed(range(8)):
            rim_copy(side).start()
    with scope("send_cache"):
        z_start(0)

    with scope("wait_weights"):
        for group in w_loads:
            for load in group:
                load.wait()
    with scope("wait_rims"):
        for side in range(8):
            rim_copy(opposite(side)).wait_recv()
        z_start(1)
    with scope("conv_first"):
        put_rims(2)
        build1(5)
        build1(4)
        put_rims(1)
        build1(3)
        build1(2)
        for a in (2, 1, 0):
            conv(0, a, (5,))
            conv(0, a, (4,))
        for f in (5, 4):
            put2(f, *finish_first(f))
        conv(0, 2, (2,))
        conv(0, 2, (3,))
        conv(0, 1, (3,), halves=True)
        build2(5)
        build2(4)
        pack_late()
    with scope("send_late"):
        z_start(2)
    with scope("conv_ahead"):
        conv(1, 2, (4, 5))
        conv(1, 1, (5,))

    with scope("wait_cache"):
        z_wait(0)
        z_wait(1)

    def add_cache():
        low, high = body_r[0:2 * PX].astype(F32), split(body_r[2 * PX:3 * PX].astype(F32))
        for i in range(2):
            put_body1(i, low[i * PX:(i + 1) * PX], high[i])
            for border in (8, 23):
                vlo[pl.ds(edge(i, 2, border), RO)] = elo1[pl.ds(at1(i, 2, border), RO, stride=EC)]
                vhi[pl.ds(edge(i, 2, border), RO)] = ehi1[pl.ds(at1(i, 2, border), RO, stride=EC)]
        put_rims(0)
        build1(1)
        build1(0)
        conv(0, 0, (3,))
        conv(0, 0, (2,))
        conv(0, 1, (2,), halves=True)

    with scope("cache"):
        pl.when(has_earlier)(add_cache)
    with scope("conv_second"):
        for f in (2, 3):
            put2(f, *finish_first(f))
        for f in (2, 3):
            build2(f)
        conv(1, 0, (4, 5))
        conv(1, 1, (3, 4))
        conv(1, 2, (2,))
        conv(1, 2, (3,))
        finish_second(4)
        finish_second(5)

    with scope("wait_late"):
        z_wait(2)
    with scope("finish_late"):
        finish_second(2)
        finish_second(3)

    with scope("drain"):
        for side in range(8):
            rim_copy(side).wait_send()

        @pl.when(has_later)
        def _():
            for k in range(3):
                z_copy(k).wait_send()


def solution(mesh):
    sizes = tuple(mesh.shape[name] for name in ("tm", "row", "col"))

    def shards(features, conv_first, conv_second, gain_first, gain_second):
        in_hbm = pl.BlockSpec(memory_space=pltpu.HBM)
        dma = pltpu.SemaphoreType.DMA
        return pl.pallas_call(
            functools.partial(kernel, sizes),
            out_shape=pltpu.VMEM(features.shape, BF),
            in_specs=[in_hbm] * 5,
            out_specs=pl.BlockSpec(memory_space=pltpu.VMEM),
            scratch_shapes=[
                pltpu.VMEM((FR, RO, CO, C), BF),
                pltpu.VMEM((2, 1, C), F32),
                pltpu.VMEM((2, 3, 3, 3, LO, C), BF),
                pltpu.VMEM((2, 3, 3, 2, 64, C), BF),
                pltpu.VMEM((2, 3, 4, 64, C), BF),
                pltpu.VMEM((EF * ER1 * EC, LO), F32),
                pltpu.VMEM((EF * ER1 * EC, LO), F32),
                pltpu.VMEM((EF * len(EDGE) * EL, LO), F32),
                pltpu.VMEM((EF * len(EDGE) * EL, LO), F32),
                pltpu.VMEM((EF * ER2 * EC, LO), F32),
                pltpu.VMEM((EF * ER2 * EC, LO), F32),
                pltpu.VMEM((EF, ER1 * CO, 5 * LO), BF),
                pltpu.VMEM((EF, SIDE, 14 * LO), BF),
                pltpu.VMEM((EF, ER2 * CO, 5 * LO), BF),
                pltpu.VMEM((FR, MAIN + SIDE, C), F32),
                pltpu.VMEM((FR, PX, C), F32),
                pltpu.VMEM((BODY, LO), BF),
                pltpu.VMEM((BODY, LO), BF),
                pltpu.VMEM((2, RIM, LO), BF),
                pltpu.VMEM((3, RIM, LO), BF),
                pltpu.VMEM((BODY, LO), BF),
                pltpu.VMEM((BODY, LO), BF),
                dma((3,)), dma((2, 3)), dma((8,)), dma((8,)), dma((3,)), dma((3,)),
            ],
            compiler_params=pltpu.CompilerParams(
                collective_id=0, has_side_effects=True, vmem_limit_bytes=60 * 1024 * 1024),
        )(features, conv_first, conv_second, gain_first.reshape(1, C), gain_second.reshape(1, C))

    return jax.shard_map(
        shards, mesh=mesh, in_specs=(P("tm", "row", "col", None), P(), P(), P(), P()),
        out_specs=P("tm", "row", "col", None), check_vma=False)
```

```python
import functools

import jax
import jax.numpy as jnp
from jax import lax
from jax.experimental import pallas as pl
from jax.experimental.pallas import tpu as pltpu
from jax.sharding import PartitionSpec as P

MESH = pl.DeviceIdType.MESH
BF = jnp.bfloat16
F32 = jnp.float32
C = 192
LO = 128
FR, RO, CO = 4, 8, 16
PX = RO * CO
EF, ER1, ER2, EC = 6, 12, 10, 32
MAIN, SIDE = ER2 * CO, 2 * CO
EDGE = (6, 7, 8, 23, 24, 25)
EL = 32
SIDES = ((-1, 0), (1, 0), (0, -1), (0, 1), (-1, -1), (-1, 1), (1, -1), (1, 1))
SPOT = ((0, 96), (96, 96), (192, 48), (240, 48), (288, 16), (304, 16), (320, 16), (336, 16))
RIM = 352
BODY = 3 * PX


def opposite(side):
    dr, dc = SIDES[side]
    return SIDES.index((-dr, -dc))


def at1(frame, row, col):
    return (frame * ER1 + row) * EC + col


def edge(frame, row, col):
    return (frame * len(EDGE) + EDGE.index(col)) * EL + row + 6


def at2(frame, row, col):
    return (frame * ER2 + row) * EC + col


def norm_act(low, high, gain_low, gain_high):
    total = jnp.sum(low * low + 0.5 * (high * high), axis=-1, keepdims=True)
    scale = lax.rsqrt(total * (1.0 / C) + 1e-06)

    def silu(values, gain):
        half = values * scale * gain
        return half + half * jnp.tanh(half)

    return silu(low, gain_low), silu(high, gain_high)


def twice(high):
    return jnp.concatenate([high, high], axis=-1)


def first_half(lines):
    return lax.broadcasted_iota(jnp.int32, (lines, LO), 1) < 64


def swap(value):
    return pltpu.roll(value, 64, 1)


def join(first, second):
    return jnp.where(first_half(first.shape[0]), first, second)


def split(value):
    mask, other = first_half(value.shape[0]), swap(value)
    return jnp.where(mask, value, other), jnp.where(mask, other, value)


def kernel(sizes, x_hbm, w1_hbm, w2_hbm, g1_hbm, g2_hbm, out,
           x, gains, wlo, whi, wti, elo1, ehi1, vlo, vhi, elo2, ehi2, taps1, sides1, taps2, sums1, sums2,
           body_s, body_r, rim_s, rim_r, late_s, late_r,
           load_sem, w_sem, rim_ss, rim_rs, z_ss, z_rs):
    n_tm, n_row, n_col = sizes
    tm, row, col = (lax.axis_index(name) for name in ("tm", "row", "col"))
    scope = jax.named_scope

    def neighbour(dr, dc):
        return (tm, lax.rem(row + (dr + n_row), n_row), lax.rem(col + (dc + n_col), n_col))

    later = (lax.rem(tm + 1, n_tm), row, col)
    earlier = (lax.rem(tm + (n_tm - 1), n_tm), row, col)
    has_later = tm < n_tm - 1
    has_earlier = tm > 0

    barrier = pltpu.get_barrier_semaphore()
    for dr, dc in SIDES:
        pl.semaphore_signal(barrier, inc=1, device_id=neighbour(dr, dc), device_id_type=MESH)

    @pl.when(has_earlier)
    def _():
        pl.semaphore_signal(barrier, inc=1, device_id=earlier, device_id_type=MESH)

    loads = [pltpu.make_async_copy(x_hbm, x, load_sem.at[0])]
    for k, g in enumerate((g1_hbm, g2_hbm)):
        loads.append(pltpu.make_async_copy(g, gains.at[k], load_sem.at[k + 1]))
    for load in loads:
        load.start()
    w_loads = []
    for k, w in enumerate((w1_hbm, w2_hbm)):
        group = [
            pltpu.make_async_copy(w.at[:, :, :, 0:128, :], wlo.at[k], w_sem.at[k, 0]),
            pltpu.make_async_copy(w.at[:, :, 0:2, 128:192, :], whi.at[k], w_sem.at[k, 1]),
            pltpu.make_async_copy(w.at[:, :, 2, 128:192, :], wti.at[k, :, 0:3], w_sem.at[k, 2]),
        ]
        for load in group:
            load.start()
        w_loads.append(group)

    wti[:, :, 3] = jnp.zeros((2, 3, 64, C), BF)

    @pl.when(jnp.logical_not(has_earlier))
    def _():
        late_r[...] = jnp.zeros((BODY, LO), BF)

    keep_row = {-1: jnp.where(row > 0, 1.0, 0.0), 1: jnp.where(row < n_row - 1, 1.0, 0.0)}
    keep_col = {-1: jnp.where(col > 0, 1.0, 0.0), 1: jnp.where(col < n_col - 1, 1.0, 0.0)}

    def side_keep(side):
        dr, dc = SIDES[side]
        if dr and dc:
            return keep_row[dr] * keep_col[dc]
        return keep_row[dr] if dr else keep_col[dc]

    def rim_copy(side):
        here, size = SPOT[side]
        there, _ = SPOT[opposite(side)]
        return pltpu.make_async_remote_copy(
            src_ref=rim_s.at[:, pl.ds(here, size)], dst_ref=rim_r.at[1:3, pl.ds(there, size)],
            send_sem=rim_ss.at[side], recv_sem=rim_rs.at[opposite(side)],
            device_id=neighbour(*SIDES[side]), device_id_type=MESH)

    def z_copy(k):
        src, dst = ((body_s, body_r), (rim_r.at[2], rim_r.at[0]), (late_s, late_r))[k]
        return pltpu.make_async_remote_copy(
            src_ref=src, dst_ref=dst, send_sem=z_ss.at[k], recv_sem=z_rs.at[k],
            device_id=later, device_id_type=MESH)

    def z_start(k):
        pl.when(has_later)(lambda: z_copy(k).start())

    def z_wait(k):
        pl.when(has_earlier)(lambda: z_copy(k).wait_recv())

    def put_body1(frame, low, high):
        for r in range(RO):
            elo1[pl.ds(at1(frame, r + 2, 8), CO)] = low[r * CO:(r + 1) * CO]
            ehi1[pl.ds(at1(frame, r + 2, 8), CO)] = high[r * CO:(r + 1) * CO]

    def pack_rims(pair):
        f = 2 + 2 * pair
        for side, (dr, dc) in enumerate(SIDES):
            spot, _ = SPOT[side]
            r = 2 if dr < 0 else RO
            c = 8 if dc < 0 else 22
            if dc == 0:
                for q in range(2):
                    for i in range(2):
                        to = spot + (2 * i + q) * CO
                        rim_s[pair, to:to + CO] = elo1[pl.ds(at1(f + i, r + q, 8), CO)].astype(BF)
                    high = join(*[ehi1[pl.ds(at1(f + i, r + q, 8), CO)] for i in range(2)])
                    to = spot + 64 + q * CO
                    rim_s[pair, to:to + CO] = high.astype(BF)
            elif dr == 0:
                outer = 0 if dc < 0 else 1
                high = []
                for i in range(2):
                    low = [elo1[pl.ds(at1(f + i, 2, c + q), RO, stride=EC)] for q in range(2)]
                    high.append([ehi1[pl.ds(at1(f + i, 2, c + q), RO, stride=EC)] for q in range(2)])
                    to = spot + i * CO
                    rim_s[pair, to:to + CO] = jnp.concatenate(low, axis=0).astype(BF)
                    vlo[pl.ds(edge(f + i, 2, c + outer), RO)] = low[outer]
                    vhi[pl.ds(edge(f + i, 2, c + outer), RO)] = high[i][outer]
                both = [join(high[0][q], high[1][q]) for q in range(2)]
                rim_s[pair, spot + 32:spot + 48] = jnp.concatenate(both, axis=0).astype(BF)
            else:
                pairs = lax.broadcasted_iota(jnp.int32, (8, LO), 0) // 2
                low = high = jnp.zeros((8, LO), F32)
                for i in range(2):
                    for q in range(2):
                        k = 2 * i + q
                        low = jnp.where(pairs == k, elo1[pl.ds(at1(f + i, r + q, c) - 2 * k, 8)], low)
                for q in range(2):
                    both = join(*[ehi1[pl.ds(at1(f + i, r + q, c) - 2 * q, 8)] for i in range(2)])
                    high = jnp.where(pairs == q, both, high)
                rim_s[pair, spot:spot + 16] = jnp.concatenate([low, high], axis=0).astype(BF)

    def put_rims(slot):
        f = 2 * slot
        for side, (dr, dc) in enumerate(SIDES):
            spot, size = SPOT[side]
            r = 0 if dr < 0 else RO + 2
            c = 6 if dc < 0 else 24
            value = rim_r[slot, spot:spot + size].astype(F32) * side_keep(side)
            near = 1 if dc < 0 else 0
            for i in range(2):
                for q in range(2):
                    k = 2 * i + q
                    if dc == 0:
                        low, high = value[k * CO:(k + 1) * CO], split(value[64:96])[i][q * CO:(q + 1) * CO]
                        elo1[pl.ds(at1(f + i, r + q, 8), CO)] = low
                        ehi1[pl.ds(at1(f + i, r + q, 8), CO)] = high
                        for line, border in ((0, 8), (CO - 1, 23)):
                            vlo[pl.ds(edge(f + i, r + q, border), 1)] = low[line:line + 1]
                            vhi[pl.ds(edge(f + i, r + q, border), 1)] = high[line:line + 1]
                    elif dr == 0:
                        low, high = value[k * RO:(k + 1) * RO], split(value[32:48])[i][q * RO:(q + 1) * RO]
                        vlo[pl.ds(edge(f + i, 2, c + q), RO)] = low
                        vhi[pl.ds(edge(f + i, 2, c + q), RO)] = high
                        if q == near:
                            elo1[pl.ds(at1(f + i, 2, c + q), RO, stride=EC)] = low
                            ehi1[pl.ds(at1(f + i, 2, c + q), RO, stride=EC)] = high
                    else:
                        low, high = value[2 * k:2 * k + 2], split(value[8:16])[i][2 * q:2 * q + 2]
                        for j in range(2):
                            vlo[pl.ds(edge(f + i, r + q, c + j), 1)] = low[j:j + 1]
                            vhi[pl.ds(edge(f + i, r + q, c + j), 1)] = high[j:j + 1]
                        elo1[pl.ds(at1(f + i, r + q, c + near), 1)] = low[near:near + 1]
                        ehi1[pl.ds(at1(f + i, r + q, c + near), 1)] = high[near:near + 1]

    def lanes(low, high, below):
        wide = jnp.concatenate(low + [join(high[0], high[1])], axis=1).astype(BF)
        return wide, join(high[2], below).astype(BF)

    def build(elo, ehi, at, rows, taps, frame):
        last = ehi[pl.ds(at(frame, rows - 1, 9), CO)]
        for r in reversed(range(rows)):
            low = [elo[pl.ds(at(frame, r, 7 + c), CO)] for c in range(3)]
            high = [ehi[pl.ds(at(frame, r, 7 + c), CO)] for c in range(2)]
            high.append(last if r == rows - 1 else ehi[pl.ds(at(frame, r, 9), CO)])
            wide, tight = lanes(low, high, last)
            last = high[2]
            taps[frame, r * CO:(r + 1) * CO, 0:512] = wide
            taps[frame, r * CO:(r + 1) * CO, 512:640] = tight

    def build1(frame):
        build(elo1, ehi1, at1, ER1, taps1, frame)
        for s in range(2):
            lines = slice(s * CO, (s + 1) * CO)
            cols = EDGE[3 * s:3 * s + 3]
            low = [[vlo[pl.ds(edge(frame, b, c), CO)] for c in cols] for b in range(3)]
            high = [[vhi[pl.ds(edge(frame, b, c), CO)] for c in cols] for b in range(3)]
            for b in range(3):
                wide, tight = lanes(low[b], high[b], high[min(b + 1, 2)][2])
                sides1[frame, lines, b * 512:(b + 1) * 512] = wide
                if b != 1:
                    sides1[frame, lines, 1536 + b * 64:1664 + b * 64] = tight

    def build2(frame):
        build(elo2, ehi2, at2, ER2, taps2, frame)

    def products(k, a, frames, pieces=1):
        taps, count = ((taps1, MAIN), (taps2, PX))[k]
        left = []
        for f in frames:
            parts = [taps[f, b * CO:b * CO + count, 0:512] for b in range(3)]
            parts += [taps[f, b * CO:b * CO + count, 512:640] for b in (0, 2)]
            left.append(jnp.concatenate(parts, axis=1))
            if k == 0:
                left.append(sides1[f])
        left = jnp.concatenate(left, axis=0)
        right = []
        for b in range(3):
            right += [wlo[k, a, b].reshape(3 * LO, C), whi[k, a, b].reshape(LO, C)]
        right = jnp.concatenate(right + [wti[k, a].reshape(2 * LO, C)], axis=0)
        size = left.shape[0] // (len(frames) * pieces)
        dots = len(frames) if pieces == 1 else pieces
        rows = left.shape[0] // (1 if pieces == 1 else pieces)
        made = [jnp.dot(left[i:i + rows], right, preferred_element_type=F32) for i in range(0, left.shape[0], rows)]
        if pieces > 1:
            return [(i * size, value) for i, value in enumerate(made)]
        return [made[0][i * size:(i + 1) * size] for i in range(dots)]

    def conv(k, a, targets, halves=False):
        sums = (sums1, sums2)[k]
        frames = [target - 2 + a for target in targets]
        if halves:
            parts = [(targets[0], here, value) for here, value in products(k, a, frames, 2)]
        else:
            parts = [(target, 0, value) for target, value in zip(targets, products(k, a, frames))]
        for target, here, part in parts:
            lines = slice(here, here + part.shape[0])
            if (k, target) in begun:
                part = part + sums[target - 2, lines]
            sums[target - 2, lines] = part
        begun.update((k, target) for target in targets)

    begun = set()

    def put2(frame, low, high):
        for r in range(ER2):
            lines = slice(r * CO, (r + 1) * CO)
            elo2[pl.ds(at2(frame, r, 8), CO)] = low[lines]
            ehi2[pl.ds(at2(frame, r, 8), CO)] = high[lines]
        for s, c in enumerate((7, 24)):
            for first, count in ((0, 8), (8, 2)):
                lines = slice(MAIN + s * CO + first, MAIN + s * CO + first + count)
                elo2[pl.ds(at2(frame, first, c), count, stride=EC)] = low[lines]
                ehi2[pl.ds(at2(frame, first, c), count, stride=EC)] = high[lines]

    def inside(value):
        parts = [value[0:CO] * keep_row[-1], value[CO:MAIN - CO], value[MAIN - CO:MAIN] * keep_row[1]]
        lines = lax.broadcasted_iota(jnp.int32, (CO, LO), 0)
        factor = jnp.where(lines == 0, keep_row[-1], jnp.where(lines == ER2 - 1, keep_row[1], 1.0))
        for s, dc in enumerate((-1, 1)):
            parts.append(value[MAIN + s * CO:MAIN + (s + 1) * CO] * (factor * keep_col[dc]))
        return jnp.concatenate(parts, axis=0)

    def finish_first(frame):
        total = sums1[frame - 2]
        low, high = norm_act(total[:, :LO], twice(total[:, LO:]), *gain[1])
        return inside(low), inside(high)

    def finish_second(frame):
        f = frame - 2
        total = sums2[f] + x[f].reshape(PX, C).astype(F32)
        if f < 2:
            low = late_r[f * PX:(f + 1) * PX].astype(F32)
            high = late_r[2 * PX:3 * PX].astype(F32)[:, f * 64:(f + 1) * 64]
            total = total + jnp.concatenate([low, high], axis=1)
        out[f] = total.astype(BF).reshape(RO, CO, C)

    def pack_late():
        last, first = products(1, 1, (5,))[0], products(1, 0, (4, 5))
        shares = [first[0] + last, first[1]]
        for i in range(2):
            late_s[i * PX:(i + 1) * PX] = shares[i][:, :LO].astype(BF)
        late_s[2 * PX:3 * PX] = jnp.concatenate([share[:, LO:] for share in shares], axis=1).astype(BF)

    with scope("load"):
        for load in loads:
            load.wait()
        gain = []
        for k in range(2):
            value = 0.5 * gains[k]
            gain.append((value[:, :LO], twice(value[:, LO:])))
    with scope("norm"):
        kept = {}
        for f in (2, 3, 0, 1):
            value = x[f].reshape(PX, C).astype(F32)
            low, high = norm_act(value[:, :LO], twice(value[:, LO:]), *gain[0])
            put_body1(f + 2, low, high)
            kept[f] = low, high
        pack_rims(1)
        pack_rims(0)
        for i in range(2):
            body_s[i * PX:(i + 1) * PX] = kept[2 + i][0].astype(BF)
        body_s[2 * PX:3 * PX] = join(kept[2][1], kept[3][1]).astype(BF)

    with scope("barrier"):
        pl.semaphore_wait(barrier, jnp.where(has_later, 9, 8))
    with scope("send_rims"):
        for side in reversed(range(8)):
            rim_copy(side).start()
    with scope("send_cache"):
        z_start(0)

    with scope("wait_rims"):
        for side in range(8):
            rim_copy(opposite(side)).wait_recv()
        z_start(1)
    with scope("build_own"):
        put_rims(1)
        build1(3)
        build1(2)
    with scope("wait_weights"):
        for group in w_loads:
            for load in group:
                load.wait()
    with scope("conv_first"):
        conv(0, 0, (5,))
        conv(0, 0, (4,))
        put_rims(2)
        build1(4)
        build1(5)
        for a in (1, 2):
            conv(0, a, (5,))
            conv(0, a, (4,))
        for f in (5, 4):
            put2(f, *finish_first(f))
        conv(0, 2, (2, 3))
        conv(0, 1, (3,))
        build2(5)
        build2(4)
        pack_late()
    with scope("send_late"):
        z_start(2)
    with scope("wait_cache"):
        z_wait(0)
        z_wait(1)

    def add_cache():
        low, high = body_r[0:2 * PX].astype(F32), split(body_r[2 * PX:3 * PX].astype(F32))
        for i in range(2):
            put_body1(i, low[i * PX:(i + 1) * PX], high[i])
            for border in (8, 23):
                vlo[pl.ds(edge(i, 2, border), RO)] = elo1[pl.ds(at1(i, 2, border), RO, stride=EC)]
                vhi[pl.ds(edge(i, 2, border), RO)] = ehi1[pl.ds(at1(i, 2, border), RO, stride=EC)]
        put_rims(0)
        build1(1)
        build1(0)
        conv(0, 0, (3,))
        conv(0, 0, (2,))
        conv(0, 1, (2,), halves=True)

    with scope("cache"):
        pl.when(has_earlier)(add_cache)
    with scope("conv_second"):
        for f in (2, 3):
            put2(f, *finish_first(f))
        conv(1, 2, (4, 5))
        conv(1, 1, (5,))
        for f in (2, 3):
            build2(f)
        conv(1, 0, (4, 5))
        conv(1, 1, (3, 4))
        conv(1, 2, (2,))
        conv(1, 2, (3,))
        finish_second(4)
        finish_second(5)

    with scope("wait_late"):
        z_wait(2)
    with scope("finish_late"):
        finish_second(2)
        finish_second(3)

    with scope("drain"):
        for side in range(8):
            rim_copy(side).wait_send()

        @pl.when(has_later)
        def _():
            for k in range(3):
                z_copy(k).wait_send()


def solution(mesh):
    sizes = tuple(mesh.shape[name] for name in ("tm", "row", "col"))

    def shards(features, conv_first, conv_second, gain_first, gain_second):
        in_hbm = pl.BlockSpec(memory_space=pltpu.HBM)
        dma = pltpu.SemaphoreType.DMA
        return pl.pallas_call(
            functools.partial(kernel, sizes),
            out_shape=pltpu.VMEM(features.shape, BF),
            in_specs=[in_hbm] * 5,
            out_specs=pl.BlockSpec(memory_space=pltpu.VMEM),
            scratch_shapes=[
                pltpu.VMEM((FR, RO, CO, C), BF),
                pltpu.VMEM((2, 1, C), F32),
                pltpu.VMEM((2, 3, 3, 3, LO, C), BF),
                pltpu.VMEM((2, 3, 3, 2, 64, C), BF),
                pltpu.VMEM((2, 3, 4, 64, C), BF),
                pltpu.VMEM((EF * ER1 * EC, LO), F32),
                pltpu.VMEM((EF * ER1 * EC, LO), F32),
                pltpu.VMEM((EF * len(EDGE) * EL, LO), F32),
                pltpu.VMEM((EF * len(EDGE) * EL, LO), F32),
                pltpu.VMEM((EF * ER2 * EC, LO), F32),
                pltpu.VMEM((EF * ER2 * EC, LO), F32),
                pltpu.VMEM((EF, ER1 * CO, 5 * LO), BF),
                pltpu.VMEM((EF, SIDE, 14 * LO), BF),
                pltpu.VMEM((EF, ER2 * CO, 5 * LO), BF),
                pltpu.VMEM((FR, MAIN + SIDE, C), F32),
                pltpu.VMEM((FR, PX, C), F32),
                pltpu.VMEM((BODY, LO), BF),
                pltpu.VMEM((BODY, LO), BF),
                pltpu.VMEM((2, RIM, LO), BF),
                pltpu.VMEM((3, RIM, LO), BF),
                pltpu.VMEM((BODY, LO), BF),
                pltpu.VMEM((BODY, LO), BF),
                dma((3,)), dma((2, 3)), dma((8,)), dma((8,)), dma((3,)), dma((3,)),
            ],
            compiler_params=pltpu.CompilerParams(
                collective_id=0, has_side_effects=True, vmem_limit_bytes=60 * 1024 * 1024),
        )(features, conv_first, conv_second, gain_first.reshape(1, C), gain_second.reshape(1, C))

    return jax.shard_map(
        shards, mesh=mesh, in_specs=(P("tm", "row", "col", None), P(), P(), P(), P()),
        out_specs=P("tm", "row", "col", None), check_vma=False)
```

```python
import functools

import jax
import jax.numpy as jnp
from jax import lax
from jax.experimental import pallas as pl
from jax.experimental.pallas import tpu as pltpu
from jax.sharding import PartitionSpec as P

MESH = pl.DeviceIdType.MESH
BF = jnp.bfloat16
F32 = jnp.float32
C = 192
LO = 128
FR, RO, CO = 4, 8, 16
PX = RO * CO
EF, ER1, ER2, EC = 6, 12, 10, 32
MAIN, SIDE = ER2 * CO, 2 * CO
EDGE = (6, 7, 8, 23, 24, 25)
EL = 32
SIDES = ((-1, 0), (1, 0), (0, -1), (0, 1), (-1, -1), (-1, 1), (1, -1), (1, 1))
SPOT = ((0, 96), (96, 96), (192, 48), (240, 48), (288, 16), (304, 16), (320, 16), (336, 16))
RIM = 352
BODY = 3 * PX


def opposite(side):
    dr, dc = SIDES[side]
    return SIDES.index((-dr, -dc))


def at1(frame, row, col):
    return (frame * ER1 + row) * EC + col


def edge(frame, row, col):
    return (frame * len(EDGE) + EDGE.index(col)) * EL + row + 6


def at2(frame, row, col):
    return (frame * ER2 + row) * EC + col


def norm_act(low, high, gain_low, gain_high):
    total = jnp.sum(low * low + 0.5 * (high * high), axis=-1, keepdims=True)
    scale = lax.rsqrt(total * (1.0 / C) + 1e-06)

    def silu(values, gain):
        half = values * scale * gain
        return half + half * jnp.tanh(half)

    return silu(low, gain_low), silu(high, gain_high)


def twice(high):
    return jnp.concatenate([high, high], axis=-1)


def first_half(lines):
    return lax.broadcasted_iota(jnp.int32, (lines, LO), 1) < 64


def swap(value):
    return pltpu.roll(value, 64, 1)


def join(first, second):
    return jnp.where(first_half(first.shape[0]), first, second)


def split(value):
    mask, other = first_half(value.shape[0]), swap(value)
    return jnp.where(mask, value, other), jnp.where(mask, other, value)


def kernel(sizes, x_hbm, w1_hbm, w2_hbm, g1_hbm, g2_hbm, out,
           x, gains, wlo, whi, wti, elo1, ehi1, vlo, vhi, elo2, ehi2, taps1, sides1, taps2, sums1, sums2,
           body_s, body_r, rim_s, rim_r, late_s, late_r,
           load_sem, w_sem, rim_ss, rim_rs, z_ss, z_rs):
    n_tm, n_row, n_col = sizes
    tm, row, col = (lax.axis_index(name) for name in ("tm", "row", "col"))
    scope = jax.named_scope

    def neighbour(dr, dc):
        return (tm, lax.rem(row + (dr + n_row), n_row), lax.rem(col + (dc + n_col), n_col))

    later = (lax.rem(tm + 1, n_tm), row, col)
    earlier = (lax.rem(tm + (n_tm - 1), n_tm), row, col)
    has_later = tm < n_tm - 1
    has_earlier = tm > 0

    up, down, left, right = row > 0, row < n_row - 1, col > 0, col < n_col - 1
    beside = (
        up, down, left, right, jnp.logical_and(up, left), jnp.logical_and(up, right),
        jnp.logical_and(down, left), jnp.logical_and(down, right))

    barrier = pltpu.get_barrier_semaphore()
    for side, (dr, dc) in enumerate(SIDES):
        @pl.when(beside[side])
        def _():
            pl.semaphore_signal(barrier, inc=1, device_id=neighbour(dr, dc), device_id_type=MESH)

    @pl.when(has_earlier)
    def _():
        pl.semaphore_signal(barrier, inc=1, device_id=earlier, device_id_type=MESH)

    loads = [pltpu.make_async_copy(x_hbm, x, load_sem.at[0])]
    for k, g in enumerate((g1_hbm, g2_hbm)):
        loads.append(pltpu.make_async_copy(g, gains.at[k], load_sem.at[k + 1]))
    for load in loads:
        load.start()
    w_loads = []
    for k, w in enumerate((w1_hbm, w2_hbm)):
        group = [
            pltpu.make_async_copy(w.at[:, :, :, 0:128, :], wlo.at[k], w_sem.at[k, 0]),
            pltpu.make_async_copy(w.at[:, :, 0:2, 128:192, :], whi.at[k], w_sem.at[k, 1]),
            pltpu.make_async_copy(w.at[:, :, 2, 128:192, :], wti.at[k, :, 0:3], w_sem.at[k, 2]),
        ]
        for load in group:
            load.start()
        w_loads.append(group)

    wti[:, :, 3] = jnp.zeros((2, 3, 64, C), BF)

    @pl.when(jnp.logical_not(has_earlier))
    def _():
        late_r[...] = jnp.zeros((BODY, LO), BF)

    keep_row = {-1: jnp.where(row > 0, 1.0, 0.0), 1: jnp.where(row < n_row - 1, 1.0, 0.0)}
    keep_col = {-1: jnp.where(col > 0, 1.0, 0.0), 1: jnp.where(col < n_col - 1, 1.0, 0.0)}

    for side in range(8):
        here, size = SPOT[side]

        @pl.when(jnp.logical_not(beside[side]))
        def _():
            rim_r[1:3, here:here + size] = jnp.zeros((2, size, LO), BF)

    def rim_copy(side):
        here, size = SPOT[side]
        there, _ = SPOT[opposite(side)]
        return pltpu.make_async_remote_copy(
            src_ref=rim_s.at[:, pl.ds(here, size)], dst_ref=rim_r.at[1:3, pl.ds(there, size)],
            send_sem=rim_ss.at[side], recv_sem=rim_rs.at[opposite(side)],
            device_id=neighbour(*SIDES[side]), device_id_type=MESH)

    def z_copy(k):
        src, dst = ((body_s, body_r), (rim_r.at[2], rim_r.at[0]), (late_s, late_r))[k]
        return pltpu.make_async_remote_copy(
            src_ref=src, dst_ref=dst, send_sem=z_ss.at[k], recv_sem=z_rs.at[k],
            device_id=later, device_id_type=MESH)

    def z_start(k):
        pl.when(has_later)(lambda: z_copy(k).start())

    def z_wait(k):
        pl.when(has_earlier)(lambda: z_copy(k).wait_recv())

    def put_body1(frame, low, high):
        for r in range(RO):
            elo1[pl.ds(at1(frame, r + 2, 8), CO)] = low[r * CO:(r + 1) * CO]
            ehi1[pl.ds(at1(frame, r + 2, 8), CO)] = high[r * CO:(r + 1) * CO]

    def pack_rims(pair):
        f = 2 + 2 * pair
        for side, (dr, dc) in enumerate(SIDES):
            spot, _ = SPOT[side]
            r = 2 if dr < 0 else RO
            c = 8 if dc < 0 else 22
            if dc == 0:
                for q in range(2):
                    for i in range(2):
                        to = spot + (2 * i + q) * CO
                        rim_s[pair, to:to + CO] = elo1[pl.ds(at1(f + i, r + q, 8), CO)].astype(BF)
                    high = join(*[ehi1[pl.ds(at1(f + i, r + q, 8), CO)] for i in range(2)])
                    to = spot + 64 + q * CO
                    rim_s[pair, to:to + CO] = high.astype(BF)
            elif dr == 0:
                outer = 0 if dc < 0 else 1
                high = []
                for i in range(2):
                    low = [elo1[pl.ds(at1(f + i, 2, c + q), RO, stride=EC)] for q in range(2)]
                    high.append([ehi1[pl.ds(at1(f + i, 2, c + q), RO, stride=EC)] for q in range(2)])
                    to = spot + i * CO
                    rim_s[pair, to:to + CO] = jnp.concatenate(low, axis=0).astype(BF)
                    vlo[pl.ds(edge(f + i, 2, c + outer), RO)] = low[outer]
                    vhi[pl.ds(edge(f + i, 2, c + outer), RO)] = high[i][outer]
                both = [join(high[0][q], high[1][q]) for q in range(2)]
                rim_s[pair, spot + 32:spot + 48] = jnp.concatenate(both, axis=0).astype(BF)
            else:
                pairs = lax.broadcasted_iota(jnp.int32, (8, LO), 0) // 2
                low = high = jnp.zeros((8, LO), F32)
                for i in range(2):
                    for q in range(2):
                        k = 2 * i + q
                        low = jnp.where(pairs == k, elo1[pl.ds(at1(f + i, r + q, c) - 2 * k, 8)], low)
                for q in range(2):
                    both = join(*[ehi1[pl.ds(at1(f + i, r + q, c) - 2 * q, 8)] for i in range(2)])
                    high = jnp.where(pairs == q, both, high)
                rim_s[pair, spot:spot + 16] = jnp.concatenate([low, high], axis=0).astype(BF)

    def put_rims(slot):
        f = 2 * slot
        for side, (dr, dc) in enumerate(SIDES):
            spot, size = SPOT[side]
            r = 0 if dr < 0 else RO + 2
            c = 6 if dc < 0 else 24
            value = rim_r[slot, spot:spot + size].astype(F32)
            near = 1 if dc < 0 else 0
            for i in range(2):
                for q in range(2):
                    k = 2 * i + q
                    if dc == 0:
                        low, high = value[k * CO:(k + 1) * CO], split(value[64:96])[i][q * CO:(q + 1) * CO]
                        elo1[pl.ds(at1(f + i, r + q, 8), CO)] = low
                        ehi1[pl.ds(at1(f + i, r + q, 8), CO)] = high
                        for line, border in ((0, 8), (CO - 1, 23)):
                            vlo[pl.ds(edge(f + i, r + q, border), 1)] = low[line:line + 1]
                            vhi[pl.ds(edge(f + i, r + q, border), 1)] = high[line:line + 1]
                    elif dr == 0:
                        low, high = value[k * RO:(k + 1) * RO], split(value[32:48])[i][q * RO:(q + 1) * RO]
                        vlo[pl.ds(edge(f + i, 2, c + q), RO)] = low
                        vhi[pl.ds(edge(f + i, 2, c + q), RO)] = high
                        if q == near:
                            elo1[pl.ds(at1(f + i, 2, c + q), RO, stride=EC)] = low
                            ehi1[pl.ds(at1(f + i, 2, c + q), RO, stride=EC)] = high
                    else:
                        low, high = value[2 * k:2 * k + 2], split(value[8:16])[i][2 * q:2 * q + 2]
                        for j in range(2):
                            vlo[pl.ds(edge(f + i, r + q, c + j), 1)] = low[j:j + 1]
                            vhi[pl.ds(edge(f + i, r + q, c + j), 1)] = high[j:j + 1]
                        elo1[pl.ds(at1(f + i, r + q, c + near), 1)] = low[near:near + 1]
                        ehi1[pl.ds(at1(f + i, r + q, c + near), 1)] = high[near:near + 1]

    def lanes(low, high, below):
        wide = jnp.concatenate(low + [join(high[0], high[1])], axis=1).astype(BF)
        return wide, join(high[2], below).astype(BF)

    def build(elo, ehi, at, rows, taps, frame):
        last = ehi[pl.ds(at(frame, rows - 1, 9), CO)]
        for r in reversed(range(rows)):
            low = [elo[pl.ds(at(frame, r, 7 + c), CO)] for c in range(3)]
            high = [ehi[pl.ds(at(frame, r, 7 + c), CO)] for c in range(2)]
            high.append(last if r == rows - 1 else ehi[pl.ds(at(frame, r, 9), CO)])
            wide, tight = lanes(low, high, last)
            last = high[2]
            taps[frame, r * CO:(r + 1) * CO, 0:512] = wide
            taps[frame, r * CO:(r + 1) * CO, 512:640] = tight

    def build1(frame):
        build(elo1, ehi1, at1, ER1, taps1, frame)
        for s in range(2):
            lines = slice(s * CO, (s + 1) * CO)
            cols = EDGE[3 * s:3 * s + 3]
            low = [[vlo[pl.ds(edge(frame, b, c), CO)] for c in cols] for b in range(3)]
            high = [[vhi[pl.ds(edge(frame, b, c), CO)] for c in cols] for b in range(3)]
            for b in range(3):
                wide, tight = lanes(low[b], high[b], high[min(b + 1, 2)][2])
                sides1[frame, lines, b * 512:(b + 1) * 512] = wide
                if b != 1:
                    sides1[frame, lines, 1536 + b * 64:1664 + b * 64] = tight

    def build2(frame):
        build(elo2, ehi2, at2, ER2, taps2, frame)

    def products(k, a, frames, pieces=1):
        taps, count = ((taps1, MAIN), (taps2, PX))[k]
        left = []
        for f in frames:
            parts = [taps[f, b * CO:b * CO + count, 0:512] for b in range(3)]
            parts += [taps[f, b * CO:b * CO + count, 512:640] for b in (0, 2)]
            left.append(jnp.concatenate(parts, axis=1))
            if k == 0:
                left.append(sides1[f])
        left = jnp.concatenate(left, axis=0)
        right = []
        for b in range(3):
            right += [wlo[k, a, b].reshape(3 * LO, C), whi[k, a, b].reshape(LO, C)]
        right = jnp.concatenate(right + [wti[k, a].reshape(2 * LO, C)], axis=0)
        size = left.shape[0] // (len(frames) * pieces)
        dots = len(frames) if pieces == 1 else pieces
        rows = left.shape[0] // (1 if pieces == 1 else pieces)
        made = [jnp.dot(left[i:i + rows], right, preferred_element_type=F32) for i in range(0, left.shape[0], rows)]
        if pieces > 1:
            return [(i * size, value) for i, value in enumerate(made)]
        return [made[0][i * size:(i + 1) * size] for i in range(dots)]

    def conv(k, a, targets, halves=False):
        sums = (sums1, sums2)[k]
        frames = [target - 2 + a for target in targets]
        if halves:
            parts = [(targets[0], here, value) for here, value in products(k, a, frames, 2)]
        else:
            parts = [(target, 0, value) for target, value in zip(targets, products(k, a, frames))]
        for target, here, part in parts:
            lines = slice(here, here + part.shape[0])
            if (k, target) in begun:
                part = part + sums[target - 2, lines]
            sums[target - 2, lines] = part
        begun.update((k, target) for target in targets)

    begun = set()

    def put2(frame, low, high):
        for r in range(ER2):
            lines = slice(r * CO, (r + 1) * CO)
            elo2[pl.ds(at2(frame, r, 8), CO)] = low[lines]
            ehi2[pl.ds(at2(frame, r, 8), CO)] = high[lines]
        for s, c in enumerate((7, 24)):
            for first, count in ((0, 8), (8, 2)):
                lines = slice(MAIN + s * CO + first, MAIN + s * CO + first + count)
                elo2[pl.ds(at2(frame, first, c), count, stride=EC)] = low[lines]
                ehi2[pl.ds(at2(frame, first, c), count, stride=EC)] = high[lines]

    def inside(value):
        parts = [value[0:CO] * keep_row[-1], value[CO:MAIN - CO], value[MAIN - CO:MAIN] * keep_row[1]]
        lines = lax.broadcasted_iota(jnp.int32, (CO, LO), 0)
        factor = jnp.where(lines == 0, keep_row[-1], jnp.where(lines == ER2 - 1, keep_row[1], 1.0))
        for s, dc in enumerate((-1, 1)):
            parts.append(value[MAIN + s * CO:MAIN + (s + 1) * CO] * (factor * keep_col[dc]))
        return jnp.concatenate(parts, axis=0)

    def finish_first(frame):
        total = sums1[frame - 2]
        low, high = norm_act(total[:, :LO], twice(total[:, LO:]), *gain[1])
        return inside(low), inside(high)

    def finish_second(frame):
        f = frame - 2
        total = sums2[f] + x[f].reshape(PX, C).astype(F32)
        if f < 2:
            low = late_r[f * PX:(f + 1) * PX].astype(F32)
            high = late_r[2 * PX:3 * PX].astype(F32)[:, f * 64:(f + 1) * 64]
            total = total + jnp.concatenate([low, high], axis=1)
        out[f] = total.astype(BF).reshape(RO, CO, C)

    def pack_late():
        last, first = products(1, 1, (5,))[0], products(1, 0, (4, 5))
        shares = [first[0] + last, first[1]]
        for i in range(2):
            late_s[i * PX:(i + 1) * PX] = shares[i][:, :LO].astype(BF)
        late_s[2 * PX:3 * PX] = jnp.concatenate([share[:, LO:] for share in shares], axis=1).astype(BF)

    with scope("load"):
        for load in loads:
            load.wait()
        gain = []
        for k in range(2):
            value = 0.5 * gains[k]
            gain.append((value[:, :LO], twice(value[:, LO:])))
    with scope("norm"):
        kept = {}
        for f in (2, 3, 0, 1):
            value = x[f].reshape(PX, C).astype(F32)
            low, high = norm_act(value[:, :LO], twice(value[:, LO:]), *gain[0])
            put_body1(f + 2, low, high)
            kept[f] = low, high
        pack_rims(1)
        pack_rims(0)
        for i in range(2):
            body_s[i * PX:(i + 1) * PX] = kept[2 + i][0].astype(BF)
        body_s[2 * PX:3 * PX] = join(kept[2][1], kept[3][1]).astype(BF)

    with scope("barrier"):
        count = jnp.where(has_later, 1, 0)
        for side in range(8):
            count = count + jnp.where(beside[side], 1, 0)
        pl.semaphore_wait(barrier, count)
    with scope("send_rims"):
        for side in reversed(range(8)):
            pl.when(beside[side])(lambda: rim_copy(side).start())
    with scope("send_cache"):
        z_start(0)

    with scope("wait_rims"):
        for side in range(8):
            pl.when(beside[side])(lambda: rim_copy(opposite(side)).wait_recv())
        z_start(1)
    with scope("build_own"):
        put_rims(1)
        build1(3)
        build1(2)
    with scope("wait_weights"):
        for group in w_loads:
            for load in group:
                load.wait()
    with scope("conv_first"):
        conv(0, 0, (5,))
        conv(0, 0, (4,))
        put_rims(2)
        build1(4)
        build1(5)
        for a in (1, 2):
            conv(0, a, (5,))
            conv(0, a, (4,))
        for f in (5, 4):
            put2(f, *finish_first(f))
        conv(0, 2, (2, 3))
        conv(0, 1, (3,))
        build2(5)
        build2(4)
        pack_late()
    with scope("send_late"):
        z_start(2)
    with scope("wait_cache"):
        z_wait(0)
        z_wait(1)

    def add_cache():
        low, high = body_r[0:2 * PX].astype(F32), split(body_r[2 * PX:3 * PX].astype(F32))
        for i in range(2):
            put_body1(i, low[i * PX:(i + 1) * PX], high[i])
            for border in (8, 23):
                vlo[pl.ds(edge(i, 2, border), RO)] = elo1[pl.ds(at1(i, 2, border), RO, stride=EC)]
                vhi[pl.ds(edge(i, 2, border), RO)] = ehi1[pl.ds(at1(i, 2, border), RO, stride=EC)]
        put_rims(0)
        build1(1)
        build1(0)
        conv(0, 0, (3,))
        conv(0, 0, (2,))
        conv(0, 1, (2,), halves=True)

    with scope("cache"):
        pl.when(has_earlier)(add_cache)
    with scope("conv_second"):
        for f in (2, 3):
            put2(f, *finish_first(f))
        conv(1, 2, (4, 5))
        conv(1, 1, (5,))
        for f in (2, 3):
            build2(f)
        conv(1, 0, (4, 5))
        conv(1, 1, (3, 4))
        conv(1, 2, (2,))
        conv(1, 2, (3,))
        finish_second(4)
        finish_second(5)

    with scope("wait_late"):
        z_wait(2)
    with scope("finish_late"):
        finish_second(2)
        finish_second(3)

    with scope("drain"):
        for side in range(8):
            pl.when(beside[side])(lambda: rim_copy(side).wait_send())

        @pl.when(has_later)
        def _():
            for k in range(3):
                z_copy(k).wait_send()


def solution(mesh):
    sizes = tuple(mesh.shape[name] for name in ("tm", "row", "col"))

    def shards(features, conv_first, conv_second, gain_first, gain_second):
        in_hbm = pl.BlockSpec(memory_space=pltpu.HBM)
        dma = pltpu.SemaphoreType.DMA
        return pl.pallas_call(
            functools.partial(kernel, sizes),
            out_shape=pltpu.VMEM(features.shape, BF),
            in_specs=[in_hbm] * 5,
            out_specs=pl.BlockSpec(memory_space=pltpu.VMEM),
            scratch_shapes=[
                pltpu.VMEM((FR, RO, CO, C), BF),
                pltpu.VMEM((2, 1, C), F32),
                pltpu.VMEM((2, 3, 3, 3, LO, C), BF),
                pltpu.VMEM((2, 3, 3, 2, 64, C), BF),
                pltpu.VMEM((2, 3, 4, 64, C), BF),
                pltpu.VMEM((EF * ER1 * EC, LO), F32),
                pltpu.VMEM((EF * ER1 * EC, LO), F32),
                pltpu.VMEM((EF * len(EDGE) * EL, LO), F32),
                pltpu.VMEM((EF * len(EDGE) * EL, LO), F32),
                pltpu.VMEM((EF * ER2 * EC, LO), F32),
                pltpu.VMEM((EF * ER2 * EC, LO), F32),
                pltpu.VMEM((EF, ER1 * CO, 5 * LO), BF),
                pltpu.VMEM((EF, SIDE, 14 * LO), BF),
                pltpu.VMEM((EF, ER2 * CO, 5 * LO), BF),
                pltpu.VMEM((FR, MAIN + SIDE, C), F32),
                pltpu.VMEM((FR, PX, C), F32),
                pltpu.VMEM((BODY, LO), BF),
                pltpu.VMEM((BODY, LO), BF),
                pltpu.VMEM((2, RIM, LO), BF),
                pltpu.VMEM((3, RIM, LO), BF),
                pltpu.VMEM((BODY, LO), BF),
                pltpu.VMEM((BODY, LO), BF),
                dma((3,)), dma((2, 3)), dma((8,)), dma((8,)), dma((3,)), dma((3,)),
            ],
            compiler_params=pltpu.CompilerParams(
                collective_id=0, has_side_effects=True, vmem_limit_bytes=60 * 1024 * 1024),
        )(features, conv_first, conv_second, gain_first.reshape(1, C), gain_second.reshape(1, C))

    return jax.shard_map(
        shards, mesh=mesh, in_specs=(P("tm", "row", "col", None), P(), P(), P(), P()),
        out_specs=P("tm", "row", "col", None), check_vma=False)
```

```python
import functools

import jax
import jax.numpy as jnp
from jax import lax
from jax.experimental import pallas as pl
from jax.experimental.pallas import tpu as pltpu
from jax.sharding import PartitionSpec as P

MESH = pl.DeviceIdType.MESH
BF = jnp.bfloat16
F32 = jnp.float32
C = 192
LO = 128
FR, RO, CO = 4, 8, 16
PX = RO * CO
EF, ER1, ER2, EC = 6, 12, 10, 32
MAIN, SIDE = ER2 * CO, 2 * CO
EDGE = (6, 7, 8, 23, 24, 25)
EL = 32
SIDES = ((-1, 0), (1, 0), (0, -1), (0, 1), (-1, -1), (-1, 1), (1, -1), (1, 1))
SPOT = ((0, 96), (96, 96), (192, 48), (240, 48), (288, 16), (304, 16), (320, 16), (336, 16))
RIM = 352
BODY = 3 * PX


def opposite(side):
    dr, dc = SIDES[side]
    return SIDES.index((-dr, -dc))


def at1(frame, row, col):
    return (frame * ER1 + row) * EC + col


def edge(frame, row, col):
    return (frame * len(EDGE) + EDGE.index(col)) * EL + row + 6


def at2(frame, row, col):
    return (frame * ER2 + row) * EC + col


def norm_act(low, high, gain_low, gain_high):
    total = jnp.sum(low * low + 0.5 * (high * high), axis=-1, keepdims=True)
    scale = lax.rsqrt(total * (1.0 / C) + 1e-06)

    def silu(values, gain):
        half = values * scale * gain
        return half + half * jnp.tanh(half)

    return silu(low, gain_low), silu(high, gain_high)


def twice(high):
    return jnp.concatenate([high, high], axis=-1)


def first_half(lines):
    return lax.broadcasted_iota(jnp.int32, (lines, LO), 1) < 64


def swap(value):
    return pltpu.roll(value, 64, 1)


def join(first, second):
    return jnp.where(first_half(first.shape[0]), first, second)


def split(value):
    mask, other = first_half(value.shape[0]), swap(value)
    return jnp.where(mask, value, other), jnp.where(mask, other, value)


def kernel(sizes, x_hbm, w1_hbm, w2_hbm, g1_hbm, g2_hbm, out,
           x, gains, wlo, whi, wti, elo1, ehi1, vlo, vhi, elo2, ehi2, taps1, sides1, taps2, sums1, sums2,
           body_s, body_r, rim_s, rim_r, late_s, late_r,
           load_sem, w_sem, rim_ss, rim_rs, z_ss, z_rs):
    n_tm, n_row, n_col = sizes
    tm, row, col = (lax.axis_index(name) for name in ("tm", "row", "col"))
    scope = jax.named_scope

    def neighbour(dr, dc):
        return (tm, lax.rem(row + (dr + n_row), n_row), lax.rem(col + (dc + n_col), n_col))

    later = (lax.rem(tm + 1, n_tm), row, col)
    earlier = (lax.rem(tm + (n_tm - 1), n_tm), row, col)
    has_later = tm < n_tm - 1
    has_earlier = tm > 0

    up, down, left, right = row > 0, row < n_row - 1, col > 0, col < n_col - 1
    beside = (
        up, down, left, right, jnp.logical_and(up, left), jnp.logical_and(up, right),
        jnp.logical_and(down, left), jnp.logical_and(down, right))

    barrier = pltpu.get_barrier_semaphore()
    for side, (dr, dc) in enumerate(SIDES):
        @pl.when(beside[side])
        def _():
            pl.semaphore_signal(barrier, inc=1, device_id=neighbour(dr, dc), device_id_type=MESH)

    @pl.when(has_earlier)
    def _():
        pl.semaphore_signal(barrier, inc=1, device_id=earlier, device_id_type=MESH)

    loads = [pltpu.make_async_copy(x_hbm, x, load_sem.at[0])]
    for k, g in enumerate((g1_hbm, g2_hbm)):
        loads.append(pltpu.make_async_copy(g, gains.at[k], load_sem.at[k + 1]))
    for load in loads:
        load.start()
    w_loads = []
    for k, w in enumerate((w1_hbm, w2_hbm)):
        group = [
            pltpu.make_async_copy(w.at[:, :, :, 0:128, :], wlo.at[k], w_sem.at[k, 0]),
            pltpu.make_async_copy(w.at[:, :, 0:2, 128:192, :], whi.at[k], w_sem.at[k, 1]),
            pltpu.make_async_copy(w.at[:, :, 2, 128:192, :], wti.at[k, :, 0:3], w_sem.at[k, 2]),
        ]
        for load in group:
            load.start()
        w_loads.append(group)

    wti[:, :, 3] = jnp.zeros((2, 3, 64, C), BF)

    @pl.when(jnp.logical_not(has_earlier))
    def _():
        late_r[...] = jnp.zeros((BODY, LO), BF)

    keep_row = {-1: jnp.where(row > 0, 1.0, 0.0), 1: jnp.where(row < n_row - 1, 1.0, 0.0)}
    keep_col = {-1: jnp.where(col > 0, 1.0, 0.0), 1: jnp.where(col < n_col - 1, 1.0, 0.0)}

    for side in range(8):
        here, size = SPOT[side]

        @pl.when(jnp.logical_not(beside[side]))
        def _():
            rim_r[1:3, here:here + size] = jnp.zeros((2, size, LO), BF)

    def rim_copy(side):
        here, size = SPOT[side]
        there, _ = SPOT[opposite(side)]
        return pltpu.make_async_remote_copy(
            src_ref=rim_s.at[:, pl.ds(here, size)], dst_ref=rim_r.at[1:3, pl.ds(there, size)],
            send_sem=rim_ss.at[side], recv_sem=rim_rs.at[opposite(side)],
            device_id=neighbour(*SIDES[side]), device_id_type=MESH)

    def z_copy(k):
        src, dst = ((body_s, body_r), (rim_r.at[2], rim_r.at[0]), (late_s, late_r))[k]
        return pltpu.make_async_remote_copy(
            src_ref=src, dst_ref=dst, send_sem=z_ss.at[k], recv_sem=z_rs.at[k],
            device_id=later, device_id_type=MESH)

    def z_start(k):
        pl.when(has_later)(lambda: z_copy(k).start())

    def z_wait(k):
        pl.when(has_earlier)(lambda: z_copy(k).wait_recv())

    def put_body1(frame, low, high):
        for r in range(RO):
            elo1[pl.ds(at1(frame, r + 2, 8), CO)] = low[r * CO:(r + 1) * CO]
            ehi1[pl.ds(at1(frame, r + 2, 8), CO)] = high[r * CO:(r + 1) * CO]

    def pack_rims(pair):
        f = 2 + 2 * pair
        for side, (dr, dc) in enumerate(SIDES):
            spot, _ = SPOT[side]
            r = 2 if dr < 0 else RO
            c = 8 if dc < 0 else 22
            if dc == 0:
                for q in range(2):
                    for i in range(2):
                        to = spot + (2 * i + q) * CO
                        rim_s[pair, to:to + CO] = elo1[pl.ds(at1(f + i, r + q, 8), CO)].astype(BF)
                    high = join(*[ehi1[pl.ds(at1(f + i, r + q, 8), CO)] for i in range(2)])
                    to = spot + 64 + q * CO
                    rim_s[pair, to:to + CO] = high.astype(BF)
            elif dr == 0:
                outer = 0 if dc < 0 else 1
                high = []
                for i in range(2):
                    low = [elo1[pl.ds(at1(f + i, 2, c + q), RO, stride=EC)] for q in range(2)]
                    high.append([ehi1[pl.ds(at1(f + i, 2, c + q), RO, stride=EC)] for q in range(2)])
                    to = spot + i * CO
                    rim_s[pair, to:to + CO] = jnp.concatenate(low, axis=0).astype(BF)
                    vlo[pl.ds(edge(f + i, 2, c + outer), RO)] = low[outer]
                    vhi[pl.ds(edge(f + i, 2, c + outer), RO)] = high[i][outer]
                both = [join(high[0][q], high[1][q]) for q in range(2)]
                rim_s[pair, spot + 32:spot + 48] = jnp.concatenate(both, axis=0).astype(BF)
            else:
                pairs = lax.broadcasted_iota(jnp.int32, (8, LO), 0) // 2
                low = high = jnp.zeros((8, LO), F32)
                for i in range(2):
                    for q in range(2):
                        k = 2 * i + q
                        low = jnp.where(pairs == k, elo1[pl.ds(at1(f + i, r + q, c) - 2 * k, 8)], low)
                for q in range(2):
                    both = join(*[ehi1[pl.ds(at1(f + i, r + q, c) - 2 * q, 8)] for i in range(2)])
                    high = jnp.where(pairs == q, both, high)
                rim_s[pair, spot:spot + 16] = jnp.concatenate([low, high], axis=0).astype(BF)

    def put_rims(slot):
        f = 2 * slot
        for side, (dr, dc) in enumerate(SIDES):
            spot, size = SPOT[side]
            r = 0 if dr < 0 else RO + 2
            c = 6 if dc < 0 else 24
            value = rim_r[slot, spot:spot + size].astype(F32)
            near = 1 if dc < 0 else 0
            for i in range(2):
                for q in range(2):
                    k = 2 * i + q
                    if dc == 0:
                        low, high = value[k * CO:(k + 1) * CO], split(value[64:96])[i][q * CO:(q + 1) * CO]
                        elo1[pl.ds(at1(f + i, r + q, 8), CO)] = low
                        ehi1[pl.ds(at1(f + i, r + q, 8), CO)] = high
                        for line, border in ((0, 8), (CO - 1, 23)):
                            vlo[pl.ds(edge(f + i, r + q, border), 1)] = low[line:line + 1]
                            vhi[pl.ds(edge(f + i, r + q, border), 1)] = high[line:line + 1]
                    elif dr == 0:
                        low, high = value[k * RO:(k + 1) * RO], split(value[32:48])[i][q * RO:(q + 1) * RO]
                        vlo[pl.ds(edge(f + i, 2, c + q), RO)] = low
                        vhi[pl.ds(edge(f + i, 2, c + q), RO)] = high
                        if q == near:
                            elo1[pl.ds(at1(f + i, 2, c + q), RO, stride=EC)] = low
                            ehi1[pl.ds(at1(f + i, 2, c + q), RO, stride=EC)] = high
                    else:
                        low, high = value[2 * k:2 * k + 2], split(value[8:16])[i][2 * q:2 * q + 2]
                        for j in range(2):
                            vlo[pl.ds(edge(f + i, r + q, c + j), 1)] = low[j:j + 1]
                            vhi[pl.ds(edge(f + i, r + q, c + j), 1)] = high[j:j + 1]
                        elo1[pl.ds(at1(f + i, r + q, c + near), 1)] = low[near:near + 1]
                        ehi1[pl.ds(at1(f + i, r + q, c + near), 1)] = high[near:near + 1]

    def lanes(low, high, below):
        wide = jnp.concatenate(low + [join(high[0], high[1])], axis=1).astype(BF)
        return wide, join(high[2], below).astype(BF)

    def build(elo, ehi, at, rows, taps, frame):
        last = ehi[pl.ds(at(frame, rows - 1, 9), CO)]
        for r in reversed(range(rows)):
            low = [elo[pl.ds(at(frame, r, 7 + c), CO)] for c in range(3)]
            high = [ehi[pl.ds(at(frame, r, 7 + c), CO)] for c in range(2)]
            high.append(last if r == rows - 1 else ehi[pl.ds(at(frame, r, 9), CO)])
            wide, tight = lanes(low, high, last)
            last = high[2]
            taps[frame, r * CO:(r + 1) * CO, 0:512] = wide
            taps[frame, r * CO:(r + 1) * CO, 512:640] = tight

    def build1(frame):
        build(elo1, ehi1, at1, ER1, taps1, frame)
        for s in range(2):
            lines = slice(s * CO, (s + 1) * CO)
            cols = EDGE[3 * s:3 * s + 3]
            low = [[vlo[pl.ds(edge(frame, b, c), CO)] for c in cols] for b in range(3)]
            high = [[vhi[pl.ds(edge(frame, b, c), CO)] for c in cols] for b in range(3)]
            for b in range(3):
                wide, tight = lanes(low[b], high[b], high[min(b + 1, 2)][2])
                sides1[frame, lines, b * 512:(b + 1) * 512] = wide
                if b != 1:
                    sides1[frame, lines, 1536 + b * 64:1664 + b * 64] = tight

    def build2(frame):
        build(elo2, ehi2, at2, ER2, taps2, frame)

    def products(k, a, frames, pieces=1):
        taps, count = ((taps1, MAIN), (taps2, PX))[k]
        left = []
        for f in frames:
            parts = [taps[f, b * CO:b * CO + count, 0:512] for b in range(3)]
            parts += [taps[f, b * CO:b * CO + count, 512:640] for b in (0, 2)]
            left.append(jnp.concatenate(parts, axis=1))
            if k == 0:
                left.append(sides1[f])
        left = jnp.concatenate(left, axis=0)
        right = []
        for b in range(3):
            right += [wlo[k, a, b].reshape(3 * LO, C), whi[k, a, b].reshape(LO, C)]
        right = jnp.concatenate(right + [wti[k, a].reshape(2 * LO, C)], axis=0)
        size = left.shape[0] // (len(frames) * pieces)
        dots = len(frames) if pieces == 1 else pieces
        rows = left.shape[0] // (1 if pieces == 1 else pieces)
        made = [jnp.dot(left[i:i + rows], right, preferred_element_type=F32) for i in range(0, left.shape[0], rows)]
        if pieces > 1:
            return [(i * size, value) for i, value in enumerate(made)]
        return [made[0][i * size:(i + 1) * size] for i in range(dots)]

    def conv(k, a, targets, halves=False):
        sums = (sums1, sums2)[k]
        frames = [target - 2 + a for target in targets]
        if halves:
            parts = [(targets[0], here, value) for here, value in products(k, a, frames, 2)]
        else:
            parts = [(target, 0, value) for target, value in zip(targets, products(k, a, frames))]
        for target, here, part in parts:
            lines = slice(here, here + part.shape[0])
            if (k, target) in begun:
                part = part + sums[target - 2, lines]
            sums[target - 2, lines] = part
        begun.update((k, target) for target in targets)

    begun = set()

    def put2(frame, low, high):
        for r in range(ER2):
            lines = slice(r * CO, (r + 1) * CO)
            elo2[pl.ds(at2(frame, r, 8), CO)] = low[lines]
            ehi2[pl.ds(at2(frame, r, 8), CO)] = high[lines]
        for s, c in enumerate((7, 24)):
            for first, count in ((0, 8), (8, 2)):
                lines = slice(MAIN + s * CO + first, MAIN + s * CO + first + count)
                elo2[pl.ds(at2(frame, first, c), count, stride=EC)] = low[lines]
                ehi2[pl.ds(at2(frame, first, c), count, stride=EC)] = high[lines]

    def inside(value):
        parts = [value[0:CO] * keep_row[-1], value[CO:MAIN - CO], value[MAIN - CO:MAIN] * keep_row[1]]
        lines = lax.broadcasted_iota(jnp.int32, (CO, LO), 0)
        factor = jnp.where(lines == 0, keep_row[-1], jnp.where(lines == ER2 - 1, keep_row[1], 1.0))
        for s, dc in enumerate((-1, 1)):
            parts.append(value[MAIN + s * CO:MAIN + (s + 1) * CO] * (factor * keep_col[dc]))
        return jnp.concatenate(parts, axis=0)

    def finish_first(frame):
        total = sums1[frame - 2]
        low, high = norm_act(total[:, :LO], twice(total[:, LO:]), *gain[1])
        return inside(low), inside(high)

    def finish_second(frame):
        f = frame - 2
        total = sums2[f] + x[f].reshape(PX, C).astype(F32)
        if f < 2:
            low = late_r[f * PX:(f + 1) * PX].astype(F32)
            high = late_r[2 * PX:3 * PX].astype(F32)[:, f * 64:(f + 1) * 64]
            total = total + jnp.concatenate([low, high], axis=1)
        out[f] = total.astype(BF).reshape(RO, CO, C)

    def pack_late():
        last, first = products(1, 1, (5,))[0], products(1, 0, (4, 5))
        shares = [first[0] + last, first[1]]
        for i in range(2):
            late_s[i * PX:(i + 1) * PX] = shares[i][:, :LO].astype(BF)
        late_s[2 * PX:3 * PX] = jnp.concatenate([share[:, LO:] for share in shares], axis=1).astype(BF)

    with scope("load"):
        for load in loads:
            load.wait()
        gain = []
        for k in range(2):
            value = 0.5 * gains[k]
            gain.append((value[:, :LO], twice(value[:, LO:])))
    with scope("norm"):
        kept = {}
        for f in (2, 3, 0, 1):
            value = x[f].reshape(PX, C).astype(F32)
            low, high = norm_act(value[:, :LO], twice(value[:, LO:]), *gain[0])
            put_body1(f + 2, low, high)
            kept[f] = low, high
        pack_rims(1)
        pack_rims(0)
        for i in range(2):
            body_s[i * PX:(i + 1) * PX] = kept[2 + i][0].astype(BF)
        body_s[2 * PX:3 * PX] = join(kept[2][1], kept[3][1]).astype(BF)

    with scope("barrier"):
        count = jnp.where(has_later, 1, 0)
        for side in range(8):
            count = count + jnp.where(beside[side], 1, 0)
        pl.semaphore_wait(barrier, count)
    with scope("send_rims"):
        for side in reversed(range(8)):
            pl.when(beside[side])(lambda: rim_copy(side).start())
    with scope("send_cache"):
        z_start(0)

    with scope("wait_rims"):
        for side in range(8):
            pl.when(beside[side])(lambda: rim_copy(opposite(side)).wait_recv())
        z_start(1)
    with scope("build_own"):
        put_rims(1)
        build1(3)
        build1(2)
    with scope("wait_weights"):
        for group in w_loads:
            for load in group:
                load.wait()
    with scope("conv_first"):
        conv(0, 0, (5,))
        conv(0, 0, (4,))
        put_rims(2)
        build1(4)
        build1(5)
        for a in (1, 2):
            conv(0, a, (5,))
            conv(0, a, (4,))
        for f in (5, 4):
            put2(f, *finish_first(f))
        conv(0, 2, (2, 3))
        conv(0, 1, (3,))
        build2(5)
        build2(4)
        pack_late()
    with scope("send_late"):
        z_start(2)
    with scope("wait_cache"):
        z_wait(0)
        z_wait(1)

    def add_cache():
        low, high = body_r[0:2 * PX].astype(F32), split(body_r[2 * PX:3 * PX].astype(F32))
        for i in range(2):
            put_body1(i, low[i * PX:(i + 1) * PX], high[i])
            for border in (8, 23):
                vlo[pl.ds(edge(i, 2, border), RO)] = elo1[pl.ds(at1(i, 2, border), RO, stride=EC)]
                vhi[pl.ds(edge(i, 2, border), RO)] = ehi1[pl.ds(at1(i, 2, border), RO, stride=EC)]
        put_rims(0)
        build1(1)
        build1(0)
        conv(0, 0, (3,))
        conv(0, 0, (2,))
        conv(0, 1, (2,), halves=True)

    with scope("cache"):
        pl.when(has_earlier)(add_cache)
    with scope("conv_second"):
        for f in (2, 3):
            put2(f, *finish_first(f))
        conv(1, 2, (4, 5))
        conv(1, 1, (5,))
        for f in (2, 3):
            build2(f)
        conv(1, 0, (4, 5))
        conv(1, 1, (3, 4))
        conv(1, 2, (2,))
        conv(1, 2, (3,))
        finish_second(4)
        finish_second(5)

    with scope("wait_late"):
        z_wait(2)
    with scope("finish_late"):
        finish_second(2)
        finish_second(3)

    with scope("drain"):
        for side in range(8):
            pl.when(beside[side])(lambda: rim_copy(side).wait_send())

        @pl.when(has_later)
        def _():
            for k in range(3):
                z_copy(k).wait_send()


def solution(mesh):
    sizes = tuple(mesh.shape[name] for name in ("tm", "row", "col"))

    def shards(features, conv_first, conv_second, gain_first, gain_second):
        in_hbm = pl.BlockSpec(memory_space=pltpu.HBM)
        dma = pltpu.SemaphoreType.DMA
        return pl.pallas_call(
            functools.partial(kernel, sizes),
            out_shape=pltpu.VMEM(features.shape, BF),
            in_specs=[in_hbm] * 5,
            out_specs=pl.BlockSpec(memory_space=pltpu.VMEM),
            scratch_shapes=[
                pltpu.VMEM((FR, RO, CO, C), BF),
                pltpu.VMEM((2, 1, C), F32),
                pltpu.VMEM((2, 3, 3, 3, LO, C), BF),
                pltpu.VMEM((2, 3, 3, 2, 64, C), BF),
                pltpu.VMEM((2, 3, 4, 64, C), BF),
                pltpu.VMEM((EF * ER1 * EC, LO), F32),
                pltpu.VMEM((EF * ER1 * EC, LO), F32),
                pltpu.VMEM((EF * len(EDGE) * EL, LO), F32),
                pltpu.VMEM((EF * len(EDGE) * EL, LO), F32),
                pltpu.VMEM(((EF + 1) * ER2 * EC, LO), F32),
                pltpu.VMEM(((EF + 1) * ER2 * EC, LO), F32),
                pltpu.VMEM((EF, ER1 * CO, 5 * LO), BF),
                pltpu.VMEM((EF, SIDE, 14 * LO), BF),
                pltpu.VMEM((EF, ER2 * CO, 5 * LO), BF),
                pltpu.VMEM((FR, MAIN + SIDE, C), F32),
                pltpu.VMEM((FR, PX, C), F32),
                pltpu.VMEM((BODY, LO), BF),
                pltpu.VMEM((BODY, LO), BF),
                pltpu.VMEM((2, RIM, LO), BF),
                pltpu.VMEM((3, RIM, LO), BF),
                pltpu.VMEM((BODY, LO), BF),
                pltpu.VMEM((BODY, LO), BF),
                dma((3,)), dma((2, 3)), dma((8,)), dma((8,)), dma((3,)), dma((3,)),
            ],
            compiler_params=pltpu.CompilerParams(
                collective_id=0, has_side_effects=True, vmem_limit_bytes=60 * 1024 * 1024),
        )(features, conv_first, conv_second, gain_first.reshape(1, C), gain_second.reshape(1, C))

    return jax.shard_map(
        shards, mesh=mesh, in_specs=(P("tm", "row", "col", None), P(), P(), P(), P()),
        out_specs=P("tm", "row", "col", None), check_vma=False)
```
